32 devices in a mesh: groups: 2 (over y), seq: 4 (over z), mp: 2 (over x), sub: 2 (over core).
Axes of the slice: x: 2, y: 2, z: 4, core: 2. Of those that a mesh axis runs over, the one named last changes fastest.
Arguments:
- video_in: bfloat16 [1024, 4096], P(('groups', 'seq'), ('mp', 'sub')), parts along dimension 0, may hold values from -6 to 6
- audio_in: bfloat16 [256, 2048], P(('groups', 'seq'), ('mp', 'sub')), parts along dimension 0, may hold values from -6 to 6
- q_self: bfloat16 [1024, 2048], P(('groups', 'seq'), ('mp', 'sub')), parts along dimension 0
- k_self: bfloat16 [1024, 2048], P(('groups', 'seq'), ('mp', 'sub')), parts along dimension 0
- v_self: bfloat16 [1024, 2048], P(('groups', 'seq'), ('mp', 'sub')), parts along dimension 0, may hold values from -6 to 6
- q_a2v: bfloat16 [1024, 1024], P(('groups', 'seq'), ('mp', 'sub')), parts along dimension 0
- k_a2v: bfloat16 [256, 1024], P(('groups', 'seq'), ('mp', 'sub')), parts along dimension 0
- v_a2v: bfloat16 [256, 1024], P(('groups', 'seq'), ('mp', 'sub')), parts along dimension 0, may hold values from -6 to 6
- q_v2a: bfloat16 [256, 1024], P(('groups', 'seq'), ('mp', 'sub')), parts along dimension 0
- k_v2a: bfloat16 [1024, 1024], P(('groups', 'seq'), ('mp', 'sub')), parts along dimension 0
- v_v2a: bfloat16 [1024, 1024], P(('groups', 'seq'), ('mp', 'sub')), parts along dimension 0, may hold values from -6 to 6
- wo_self: bfloat16 [2048, 4096], P(('mp', 'sub')), may hold values from -0.125 to 0.125
- wo_a2v: bfloat16 [1024, 4096], P(('mp', 'sub')), may hold values from -0.1875 to 0.1875
- wo_v2a: bfloat16 [1024, 2048], P(('mp', 'sub')), may hold values from -0.1875 to 0.1875
- video_gates: bfloat16 [16, 2, 4096], replicated, may hold values from -4 to 4
- audio_gates: bfloat16 [16, 2048], replicated, may hold values from -4 to 4
- video_steps: int32 [1024], P(('groups', 'seq')), parts along dimension 0, may hold values from 0 to 15
- audio_steps: int32 [256], P(('groups', 'seq')), parts along dimension 0, may hold values from 0 to 15
- audio_len: int32 [2], P('groups'), parts along dimension 0, may hold values from 64 to 128
Outputs:
- video_out: bfloat16 [1024, 4096], P(('groups', 'seq'), ('mp', 'sub')), parts along dimension 0
- audio_out: bfloat16 [256, 2048], P(('groups', 'seq'), ('mp', 'sub')), parts along dimension 0
The draws below stay inside these ranges and needn't reach their ends.
There are 2 independent parts, one for each index of `groups`. The reference program is written for one: setup_inputs(seed, part) draws one part's arguments, and reference() takes and returns one part's arrays. A program takes and returns all parts, laid end to end along the dimension named above; an argument that names none is the same for every part. Nothing has to cross between parts.
Inputs may be any that keep to these rules, and one draw needn't show every extreme that they name: Audio tokens 0 to audio_len[0] - 1 are real, the rest are padding.
All inputs are finite; a program needn't handle non-finite values.
Results may differ from the reference program's by a relative error of at most 0.0075.
Values may be sent and summed in bfloat16 or wider, within the bound.
A program may use at most 64 MiB of HBM per device.

```python
import math
import jax
import jax.numpy as jnp
from jax import lax

DV = 4096
DA = 2048
DHV = 128
DHC = 64
HV = 16
HC = 16
NT = 16
LV = 512
LA = 128


def paired_draw(key, tag, q_rows, k_rows, heads, width):
    base = jax.random.fold_in(key, tag)
    key_q, key_k = jax.random.split(base, 2)
    cols = heads * width
    queries = jnp.clip(1.5 * jax.random.normal(key_q, (q_rows, cols), jnp.float32), -9.0, 9.0)
    keys = jnp.clip(1.5 * jax.random.normal(key_k, (k_rows, cols), jnp.float32), -9.0, 9.0)
    return (queries, keys)


def draw_q_self(key, part):
    return paired_draw(key, 11, LV, LV, HV, DHV)[0].astype(jnp.bfloat16)


def draw_k_self(key, part):
    return paired_draw(key, 11, LV, LV, HV, DHV)[1].astype(jnp.bfloat16)


def draw_q_a2v(key, part):
    return paired_draw(key, 12, LV, LA, HC, DHC)[0].astype(jnp.bfloat16)


def draw_k_a2v(key, part):
    return paired_draw(key, 12, LV, LA, HC, DHC)[1].astype(jnp.bfloat16)


def draw_q_v2a(key, part):
    return paired_draw(key, 13, LA, LV, HC, DHC)[0].astype(jnp.bfloat16)


def draw_k_v2a(key, part):
    return paired_draw(key, 13, LA, LV, HC, DHC)[1].astype(jnp.bfloat16)


def touch_ends(entries, rng, low, high):
    index_at = [jax.random.randint(jax.random.fold_in(rng, axis), (), 0, length) for axis, length in enumerate(entries.shape)]
    main_axis = entries.shape.index(max(entries.shape))
    beside = index_at[:main_axis] + [(index_at[main_axis] + 1) % entries.shape[main_axis]] + index_at[main_axis + 1:]
    return entries.at[tuple(index_at)].set(low).at[tuple(beside)].set(high)


def block_levels(stream_key, extent, cuts, least, top_value):
    gain, own = 1.0, jax.random.fold_in(stream_key, 6)
    for position, parts in cuts:
        steps = jnp.exp(jax.random.uniform(jax.random.fold_in(own, position), (parts,), jnp.float32, least / len(cuts), top_value / len(cuts)))
        gain = gain * jnp.repeat(steps, extent[position] // parts).reshape([-1 if axis == position else 1 for axis in range(len(extent))])
    return gain


def noise(stream_key, dims, spread, most, shards=(), kind=jnp.bfloat16):
    values = jax.random.normal(stream_key, dims, jnp.float32) * spread
    if len(shards) > 0:
        values = block_levels(stream_key, dims, shards, -0.22, 0.18) * values
    return jnp.clip(values, min=-most, max=most).astype(kind)


def setup_inputs(seed: int = 0, part: int = 0) -> dict:
    key_of = jax.random.split(jax.random.key(seed), 20)
    part_keys = jax.random.split(jax.random.fold_in(key_of[19], part), 20)
    return {
        "video_in": noise(part_keys[0], (LV, DV), 1.0, 6.0, ((0, 4), (1, 4))),
        "audio_in": noise(part_keys[1], (LA, DA), 1.0, 6.0, ((0, 4), (1, 4))),
        "q_self": draw_q_self(jax.random.fold_in(jax.random.fold_in(key_of[19], part), 71), part),
        "k_self": draw_k_self(jax.random.fold_in(jax.random.fold_in(key_of[19], part), 71), part),
        "v_self": noise(part_keys[4], (LV, HV * DHV), 1.0, 6.0, ((0, 4), (1, 4))),
        "q_a2v": draw_q_a2v(jax.random.fold_in(jax.random.fold_in(key_of[19], part), 71), part),
        "k_a2v": draw_k_a2v(jax.random.fold_in(jax.random.fold_in(key_of[19], part), 71), part),
        "v_a2v": noise(part_keys[7], (LA, HC * DHC), 1.0, 6.0, ((0, 4), (1, 4))),
        "q_v2a": draw_q_v2a(jax.random.fold_in(jax.random.fold_in(key_of[19], part), 71), part),
        "k_v2a": draw_k_v2a(jax.random.fold_in(jax.random.fold_in(key_of[19], part), 71), part),
        "v_v2a": noise(part_keys[10], (LV, HC * DHC), 1.0, 6.0, ((0, 4), (1, 4))),
        "wo_self": noise(key_of[11], (HV * DHV, DV), (HV * DHV) ** -0.5, 0.125, ((0, 4),)),
        "wo_a2v": noise(key_of[12], (HC * DHC, DV), (HC * DHC) ** -0.5, 0.1875, ((0, 4),)),
        "wo_v2a": noise(key_of[13], (HC * DHC, DA), (HC * DHC) ** -0.5, 0.1875, ((0, 4),)),
        "video_gates": noise(key_of[14], (NT, 2, DV), 1.0, 4.0),
        "audio_gates": noise(key_of[15], (NT, DA), 1.0, 4.0),
        "video_steps": touch_ends(jax.random.randint(part_keys[16], (LV,), 0, NT), jax.random.fold_in(part_keys[16], 1), 0, NT - 1).astype(jnp.int32),
        "audio_steps": touch_ends(jax.random.randint(part_keys[17], (LA,), 0, NT), jax.random.fold_in(part_keys[17], 1), 0, NT - 1).astype(jnp.int32),
        "audio_len": jax.random.randint(part_keys[18], (1,), LA // 2, LA + 1).astype(jnp.int32),
    }


def attend(queries, keys, values, heads, width, valid):
    rows_q = queries.shape[0]
    rows_k = keys.shape[0]
    q_heads = queries.reshape(rows_q, heads, width).transpose(1, 0, 2)
    k_heads = keys.reshape(rows_k, heads, width).transpose(1, 0, 2)
    v_heads = values.reshape(rows_k, heads, width).transpose(1, 0, 2)
    block = math.gcd(rows_q, 512)

    def one_head(triple):
        q_one, k_one, v_one = triple
        blocks = q_one.reshape(rows_q // block, block, width)

        def one_block(q_rows):
            scores = jnp.dot(q_rows, k_one.T, preferred_element_type=jnp.float32) / math.sqrt(width)
            scores = jnp.where(valid[None, :], scores, -jnp.inf)
            peak = lax.optimization_barrier(jnp.max(scores, axis=1, keepdims=True))
            weights = jnp.exp(scores - peak)
            total = lax.optimization_barrier(jnp.sum(weights, axis=1, keepdims=True))
            summed = jnp.dot(weights.astype(jnp.bfloat16), v_one, preferred_element_type=jnp.float32)
            return summed / total
        return lax.map(one_block, blocks).reshape(rows_q, width)
    result = lax.map(one_head, (q_heads, k_heads, v_heads))
    return result.transpose(1, 0, 2).reshape(rows_q, heads * width).astype(jnp.bfloat16)

def reference(video_in, audio_in, q_self, k_self, v_self, q_a2v, k_a2v, v_a2v, q_v2a, k_v2a, v_v2a, wo_self, wo_a2v, wo_v2a, video_gates, audio_gates, video_steps, audio_steps, audio_len):
    limit = audio_len[0]
    every_video = jnp.ones((LV,), dtype=bool)
    audio_valid = jnp.arange(LA, dtype=jnp.int32) < limit
    self_att = attend(q_self, k_self, v_self, HV, DHV, every_video)
    a2v_att = attend(q_a2v, k_a2v, v_a2v, HC, DHC, audio_valid)
    v2a_att = attend(q_v2a, k_v2a, v_v2a, HC, DHC, every_video)
    video_gain = video_gates[video_steps].astype(jnp.float32)
    audio_gain = audio_gates[audio_steps].astype(jnp.float32)
    present = audio_valid.astype(jnp.float32)
    video_sum = video_gain[:, 0, :] * jnp.dot(self_att, wo_self, preferred_element_type=jnp.float32)
    video_sum = video_sum + video_gain[:, 1, :] * jnp.dot(a2v_att, wo_a2v, preferred_element_type=jnp.float32)
    audio_sum = present[:, None] * audio_gain * jnp.dot(v2a_att, wo_v2a, preferred_element_type=jnp.float32)
    video_out = (video_in.astype(jnp.float32) + video_sum).astype(jnp.bfloat16)
    audio_out = (audio_in.astype(jnp.float32) + audio_sum).astype(jnp.bfloat16)
    return (video_out, audio_out)
```

```python
import functools
import math

import jax
import jax.numpy as jnp
from jax import lax
from jax.experimental import pallas as pl
from jax.experimental.pallas import tpu as pltpu
from jax.sharding import PartitionSpec as P

DHV = 128
DHC = 64
NT = 16


def start_state(rows, heads, width):
    return (
        jnp.full((rows, heads), -1e30, jnp.float32),
        jnp.zeros((rows, heads), jnp.float32),
        jnp.zeros((rows, heads, width), jnp.float32),
    )


def update_block(state, queries, keys, values, heads, width, allowed):
    rows = queries.shape[0]
    count = keys.shape[0]
    q_heads = queries.reshape(rows, heads, width)
    k_heads = keys.reshape(count, heads, width)
    v_heads = values.reshape(count, heads, width)
    scores = jnp.einsum(
        "qhd,khd->qhk", q_heads, k_heads, preferred_element_type=jnp.float32
    ) / math.sqrt(width)
    if allowed is not None:
        scores = jnp.where(allowed[None, None, :], scores, -jnp.inf)
    peak_old, total_old, summed_old = state
    peak = jnp.maximum(peak_old, jnp.max(scores, axis=2))
    weights = jnp.exp(scores - peak[:, :, None])
    factor = jnp.exp(peak_old - peak)
    total = total_old * factor + jnp.sum(weights, axis=2)
    summed = summed_old * factor[:, :, None] + jnp.einsum(
        "qhk,khd->qhd", weights.astype(jnp.bfloat16), v_heads, preferred_element_type=jnp.float32
    )
    return (peak, total, summed)


def update_state(state, queries, keys, values, heads, width, start, limit):
    count = keys.shape[0]
    block = 1024 if count > 1024 and count % 1024 == 0 else count
    if block == count:
        allowed = None
        if limit is not None:
            allowed = jnp.arange(count, dtype=jnp.int32) < limit
        return update_block(state, queries, keys, values, heads, width, allowed)
    steps = count // block
    key_blocks = keys.reshape(steps, block, keys.shape[1])
    value_blocks = values.reshape(steps, block, values.shape[1])
    offsets = jnp.arange(steps, dtype=jnp.int32) * block

    def one_block(carry, items):
        key_rows, value_rows, offset = items
        allowed = None
        if limit is not None:
            allowed = start + offset + jnp.arange(block, dtype=jnp.int32) < limit
        return (update_block(carry, queries, key_rows, value_rows, heads, width, allowed), None)

    result, _ = lax.scan(one_block, state, (key_blocks, value_blocks, offsets))
    return result


def finish(state, heads, width):
    peak, total, summed = state
    rows = summed.shape[0]
    return (summed / total[:, :, None]).reshape(rows, heads * width).astype(jnp.bfloat16)


MESH = pl.DeviceIdType.MESH
BF16 = jnp.bfloat16
F32 = jnp.float32
CHUNKS = 4


def fits(mesh, q_self, q_a2v, k_a2v):
    seq = mesh.shape["seq"]
    return (
        seq > 1
        and q_self.shape[1] == seq * DHV
        and q_a2v.shape[1] == seq * DHC
        and 2 * DHC == DHV
        and seq % 2 == 0
        and k_a2v.shape[0] % 32 == 0
        and seq * q_self.shape[0] <= 1024
        and mesh.shape["sub"] == 2
        and mesh.shape["mp"] > 1
    )


def attend(queries, keys, values, width, allowed=None):
    scores = lax.dot_general(
        queries, keys, (((1,), (1,)), ((), ())), preferred_element_type=F32
    )
    if allowed is not None:
        scores = jnp.where(allowed, scores, -jnp.inf)
    peak = jnp.max(scores, axis=1, keepdims=True)
    weights = jnp.exp2((scores - peak) * (math.log2(math.e) / math.sqrt(width)))
    total = jnp.sum(weights, axis=1, keepdims=True)
    summed = jnp.dot(weights.astype(BF16), values, preferred_element_type=F32)
    return summed / total


def spread(hot, table):
    return lax.dot_general(hot, table, (((0,), (0,)), ((), ())), preferred_element_type=F32)


def kernel(
    seq,
    mp,
    video_in,
    audio_in,
    q_self,
    k_self,
    v_self,
    q_a2v,
    k_a2v,
    v_a2v,
    q_v2a,
    k_v2a,
    v_v2a,
    wo_self,
    wo_a2v,
    wo_v2a,
    video_gates,
    audio_gates,
    video_steps,
    audio_steps,
    audio_len,
    video_out,
    audio_out,
    qs,
    ks,
    vs,
    qa,
    ka,
    va,
    qv_in,
    kv_in,
    vv_in,
    q_pack,
    kv_pack,
    q_got,
    kv_got,
    os_send,
    os,
    ov_send,
    ov_got,
    ws,
    wa,
    wv,
    vg,
    ag,
    vin,
    ain,
    gain,
    term,
    core_send,
    core_got,
    kept,
    mp_send,
    mp_got,
    acore_send,
    acore_got,
    akept,
    amp_send,
    amp_got,
    local_sem,
    seq_send_sem,
    seq_recv_sem,
    core_send_sem,
    core_recv_sem,
    mp_send_sem,
    mp_recv_sem,
):
    me = lax.axis_index("seq")
    my_mp = lax.axis_index("mp")
    my_sub = lax.axis_index("sub")
    rows = q_self.shape[0]
    arows = k_a2v.shape[0]
    width_v = wo_self.shape[1]
    width_a = wo_v2a.shape[1]
    owned_v = width_v // (2 * mp)
    owned_a = width_a // (2 * mp)
    part = owned_v // CHUNKS

    def at(index, size):
        return pl.ds(pl.multiple_of(index * size, size), size)

    def peer(d):
        return lax.rem(me + d, seq)

    def other_mp(d):
        return lax.rem(my_mp + d, mp)

    local = []

    def bring(source, target):
        copy = pltpu.make_async_copy(source, target, local_sem.at[len(local)])
        copy.start()
        local.append(copy)
        return copy

    cross = [
        bring(q_v2a, qv_in),
        bring(k_v2a, kv_in),
        bring(v_v2a, vv_in),
    ]
    first = [
        bring(video_gates, vg),
        bring(q_a2v, qa),
        bring(k_a2v, ka.at[at(me, arows)]),
        bring(v_a2v, va.at[at(me, arows)]),
        bring(wo_a2v, wa),
    ]
    own = [
        bring(q_self.at[:, at(me, DHV)], qs.at[at(me, rows)]),
        bring(k_self.at[:, at(me, DHV)], ks.at[at(me, rows)]),
        bring(v_self.at[:, at(me, DHV)], vs.at[at(me, rows)]),
    ]
    late = [
        bring(wo_self, ws),
        bring(wo_v2a, wv),
        bring(audio_gates, ag),
        bring(video_in, vin),
        bring(audio_in, ain),
    ]

    barrier = pltpu.get_barrier_semaphore()
    for d in range(1, seq):
        pl.semaphore_signal(barrier, inc=1, device_id={"seq": peer(d)}, device_id_type=MESH)
    pl.semaphore_signal(barrier, inc=1, device_id={"sub": 1 - my_sub}, device_id_type=MESH)
    for d in range(1, mp):
        pl.semaphore_signal(barrier, inc=1, device_id={"mp": other_mp(d)}, device_id_type=MESH)
    pl.semaphore_wait(barrier, seq - 1 + 1 + mp - 1)

    sent = []

    def to_seq(kind, d, source, target):
        copy = pltpu.make_async_remote_copy(
            src_ref=source,
            dst_ref=target,
            send_sem=seq_send_sem.at[kind, d],
            recv_sem=seq_recv_sem.at[kind, d],
            device_id={"seq": peer(d)},
            device_id_type=MESH,
        )
        copy.start()
        sent.append(copy)
        return copy

    order = [d for d in range(1, seq)]
    self_in = []
    for kind, (source, target) in enumerate(((k_self, ks), (q_self, qs), (v_self, vs))):
        for d in order:
            self_in.append(
                to_seq(kind, d, source.at[:, at(peer(d), DHV)], target.at[at(me, rows)])
            )
    a2v_in = []
    for kind, (source, target) in enumerate(((k_a2v, ka), (v_a2v, va))):
        for d in order:
            a2v_in.append(to_seq(3 + kind, d, source, target.at[at(me, arows)]))

    for copy in cross:
        copy.wait()
    half = arows // 2
    for h in range(seq):
        cols = slice(h * DHC, (h + 1) * DHC)
        kv = jnp.concatenate(
            [kv_in[:, cols].astype(F32), vv_in[:, cols].astype(F32)], axis=1
        ).astype(BF16)
        qh = qv_in[:, cols].astype(F32)
        kv_pack[h] = kv
        q_pack[h] = jnp.concatenate([qh[:half], qh[half:]], axis=1).astype(BF16)
    v2a_in = []
    for d in order:
        v2a_in.append(to_seq(5, d, q_pack.at[peer(d)], q_got.at[me]))
        v2a_in.append(to_seq(6, d, kv_pack.at[peer(d)], kv_got.at[at(me, rows)]))
    q_got[me] = q_pack[me]
    kv_got[at(me, rows), :] = kv_pack[me]

    for copy in first:
        copy.wait()
    levels2 = vg.shape[0]
    picks = lax.broadcasted_iota(jnp.int32, (levels2, rows), 0)
    steps2 = video_steps[...] * 2
    hot_self = (picks == steps2).astype(F32).astype(BF16)
    hot_a2v = (picks == steps2 + 1).astype(F32).astype(BF16)
    tile = min(512, width_v)
    for c in range(width_v // tile):
        cols = slice(c * tile, (c + 1) * tile)
        gain[:, cols] = spread(hot_self, vg[:, cols]).astype(BF16)
    for copy in a2v_in:
        copy.wait_recv()
    count = seq * arows
    limit = audio_len[0]
    allowed = lax.broadcasted_iota(jnp.int32, (2 * rows, count), 1) < limit
    low = lax.broadcasted_iota(jnp.int32, (rows, 2 * DHC), 1) < DHC
    pieces = []
    for pair in range(seq // 2):
        cols = slice(pair * 2 * DHC, (pair + 1) * 2 * DHC)
        qp = qa[:, cols]
        zero = jnp.zeros_like(qp)
        both = jnp.concatenate([jnp.where(low, qp, zero), jnp.where(low, zero, qp)], axis=0)
        out = attend(both, ka[:, cols], va[:, cols], DHC, allowed)
        pieces.append(jnp.where(low, out[:rows], out[rows:]).astype(BF16))
    a2v_att = jnp.concatenate(pieces, axis=1)
    for c in range(width_v // tile):
        cols = slice(c * tile, (c + 1) * tile)
        term[:, cols] = spread(hot_a2v, vg[:, cols]) * jnp.dot(
            a2v_att, wa[:, cols], preferred_element_type=F32
        )

    for copy in own:
        copy.wait()
    for copy in self_in:
        copy.wait_recv()
    self_back = []
    for d in order + [0]:
        out = attend(qs[at(peer(d), rows), :], ks[...], vs[...], DHV).astype(BF16)
        if d == 0:
            os[:, at(me, DHV)] = out
        else:
            os_send[d] = out
            self_back.append(to_seq(7, d, os_send.at[d], os.at[:, at(me, DHV)]))

    for copy in v2a_in:
        copy.wait_recv()
    blocks = []
    for p in range(seq):
        got = q_got[p].astype(F32)
        blocks.append(got[:, :DHC])
        blocks.append(got[:, DHC:])
    qv = jnp.concatenate(blocks, axis=0)
    qv = jnp.concatenate([qv, jnp.zeros_like(qv)], axis=1).astype(BF16)
    out = attend(qv, kv_got[...], kv_got[...], DHC)[:, DHC:]
    for p in range(seq):
        top = out[p * arows : p * arows + half]
        bottom = out[p * arows + half : (p + 1) * arows]
        ov_send[p] = jnp.concatenate([top, bottom], axis=1).astype(BF16)
    v2a_back = []
    for d in order:
        v2a_back.append(to_seq(8, d, ov_send.at[peer(d)], ov_got.at[me]))
    ov_got[me] = ov_send[me]

    for copy in late:
        copy.wait()
    for copy in self_back:
        copy.wait_recv()
    self_att = os[...]

    def owner(m, s):
        return 2 * m + s

    def video_part(m, s, c):
        cols = pl.ds(pl.multiple_of(owner(m, s) * owned_v + c * part, part), part)
        return term[:, cols] + gain[:, cols].astype(F32) * jnp.dot(
            self_att, ws[:, cols], preferred_element_type=F32
        )

    def to_core(c, source, target):
        copy = pltpu.make_async_remote_copy(
            src_ref=source,
            dst_ref=target,
            send_sem=core_send_sem.at[c],
            recv_sem=core_recv_sem.at[c],
            device_id={"sub": 1 - my_sub},
            device_id_type=MESH,
        )
        copy.start()
        sent.append(copy)
        return copy

    def to_mp(c, d, source, target):
        copy = pltpu.make_async_remote_copy(
            src_ref=source,
            dst_ref=target,
            send_sem=mp_send_sem.at[c, d],
            recv_sem=mp_recv_sem.at[c, d],
            device_id={"mp": other_mp(d)},
            device_id_type=MESH,
        )
        copy.start()
        sent.append(copy)
        return copy

    core_copies = {}
    mp_copies = {}

    def pass_on(c):
        core_copies[c].wait_recv()
        for d in range(1, mp):
            mp_send[c, d] = (kept[c, d] + core_got[c, d].astype(F32)).astype(BF16)
            mp_copies[c, d] = to_mp(c, d, mp_send.at[c, d], mp_got.at[c, d])
        kept[c, 0] = kept[c, 0] + core_got[c, 0].astype(F32)

    for c in range(CHUNKS):
        for d in range(mp):
            core_send[c, d] = video_part(other_mp(d), 1 - my_sub, c).astype(BF16)
        core_copies[c] = to_core(c, core_send.at[c], core_got.at[c])
        for d in range(mp):
            kept[c, d] = video_part(other_mp(d), my_sub, c)
        if c > 0:
            pass_on(c - 1)
    pass_on(CHUNKS - 1)

    for copy in v2a_back:
        copy.wait_recv()
    blocks = []
    for h in range(seq):
        got = ov_got[h].astype(F32)
        blocks.append(jnp.concatenate([got[:, :DHC], got[:, DHC:]], axis=0))
    v2a_att = jnp.concatenate(blocks, axis=1).astype(BF16)
    apicks = lax.broadcasted_iota(jnp.int32, (ag.shape[0], arows), 0)
    hot_audio = (apicks == audio_steps[...]).astype(F32).astype(BF16)
    positions = me * arows + lax.broadcasted_iota(jnp.int32, (arows, owned_a), 0)
    present = (positions < limit).astype(F32)

    def audio_part(m, s):
        cols = at(owner(m, s), owned_a)
        return (
            present
            * spread(hot_audio, ag[:, cols])
            * jnp.dot(v2a_att, wv[:, cols], preferred_element_type=F32)
        )

    for d in range(mp):
        acore_send[d] = audio_part(other_mp(d), 1 - my_sub).astype(BF16)
    acore = to_core(CHUNKS, acore_send, acore_got)
    for d in range(mp):
        akept[d] = audio_part(other_mp(d), my_sub)
    acore.wait_recv()
    for d in range(1, mp):
        amp_send[d] = (akept[d] + acore_got[d].astype(F32)).astype(BF16)
        mp_copies[CHUNKS, d] = to_mp(CHUNKS, d, amp_send.at[d], amp_got.at[d])

    for c in range(CHUNKS):
        cols = slice(c * part, (c + 1) * part)
        total = kept[c, 0]
        for d in range(1, mp):
            mp_copies[c, d].wait_recv()
            total = total + mp_got[c, d].astype(F32)
        video_out[:, cols] = (vin[:, cols].astype(F32) + total).astype(BF16)
    total = akept[0] + acore_got[0].astype(F32)
    for d in range(1, mp):
        mp_copies[CHUNKS, d].wait_recv()
        total = total + amp_got[d].astype(F32)
    audio_out[...] = (ain[...].astype(F32) + total).astype(BF16)
    for copy in sent:
        copy.wait_send()


def fused(mesh, *args):
    (
        video_in,
        audio_in,
        q_self,
        _,
        _,
        q_a2v,
        k_a2v,
        _,
        q_v2a,
        k_v2a,
        _,
        wo_self,
        wo_a2v,
        wo_v2a,
        video_gates,
        audio_gates,
        video_steps,
        audio_steps,
        _,
    ) = args
    seq, mp = mesh.shape["seq"], mesh.shape["mp"]
    rows, arows = q_self.shape[0], k_a2v.shape[0]
    args = list(args)
    levels = video_gates.shape[0]
    table = video_gates.reshape(2 * levels, video_gates.shape[2])
    args[14] = table
    args[16] = video_steps.reshape(1, rows)
    args[17] = audio_steps.reshape(1, arows)
    part = video_in.shape[1] // CHUNKS
    owned_a = audio_in.shape[1]

    def buffer(*shape, dtype=BF16):
        return pltpu.VMEM(shape, dtype)

    like = lambda array: pltpu.VMEM(array.shape, array.dtype)
    scratch = [
        buffer(seq * rows, DHV),
        buffer(seq * rows, DHV),
        buffer(seq * rows, DHV),
        like(q_a2v),
        buffer(seq * arows, seq * DHC),
        buffer(seq * arows, seq * DHC),
        like(q_v2a),
        like(k_v2a),
        like(k_v2a),
        buffer(seq, arows // 2, 2 * DHC),
        buffer(seq, rows, 2 * DHC),
        buffer(seq, arows // 2, 2 * DHC),
        buffer(seq * rows, 2 * DHC),
        buffer(seq, rows, DHV),
        buffer(rows, seq * DHV),
        buffer(seq, arows // 2, 2 * DHC),
        buffer(seq, arows // 2, 2 * DHC),
        like(wo_self),
        like(wo_a2v),
        like(wo_v2a),
        like(table),
        like(audio_gates),
        like(video_in),
        like(audio_in),
        buffer(rows, wo_self.shape[1]),
        buffer(rows, wo_self.shape[1], dtype=F32),
        buffer(CHUNKS, mp, rows, part),
        buffer(CHUNKS, mp, rows, part),
        buffer(CHUNKS, mp, rows, part, dtype=F32),
        buffer(CHUNKS, mp, rows, part),
        buffer(CHUNKS, mp, rows, part),
        buffer(mp, arows, owned_a),
        buffer(mp, arows, owned_a),
        buffer(mp, arows, owned_a, dtype=F32),
        buffer(mp, arows, owned_a),
        buffer(mp, arows, owned_a),
        pltpu.SemaphoreType.DMA((16,)),
        pltpu.SemaphoreType.DMA((9, seq)),
        pltpu.SemaphoreType.DMA((9, seq)),
        pltpu.SemaphoreType.DMA((CHUNKS + 1,)),
        pltpu.SemaphoreType.DMA((CHUNKS + 1,)),
        pltpu.SemaphoreType.DMA((CHUNKS + 1, mp)),
        pltpu.SemaphoreType.DMA((CHUNKS + 1, mp)),
    ]
    anywhere = pl.BlockSpec(memory_space=pl.ANY)
    vmem = pl.BlockSpec(memory_space=pltpu.VMEM)
    smem = pl.BlockSpec(memory_space=pltpu.SMEM)
    return pl.pallas_call(
        functools.partial(kernel, seq, mp),
        out_shape=(
            jax.ShapeDtypeStruct(video_in.shape, video_in.dtype),
            jax.ShapeDtypeStruct(audio_in.shape, audio_in.dtype),
        ),
        in_specs=[anywhere] * 16 + [vmem, vmem, smem],
        out_specs=(vmem, vmem),
        scratch_shapes=scratch,
        compiler_params=pltpu.CompilerParams(
            collective_id=0, has_side_effects=True, vmem_limit_bytes=40 * 1024 * 1024
        ),
    )(*args)


def on_device(
    mesh,
    video_in,
    audio_in,
    q_self,
    k_self,
    v_self,
    q_a2v,
    k_a2v,
    v_a2v,
    q_v2a,
    k_v2a,
    v_v2a,
    wo_self,
    wo_a2v,
    wo_v2a,
    video_gates,
    audio_gates,
    video_steps,
    audio_steps,
    audio_len,
):
    if fits(mesh, q_self, q_a2v, k_a2v):
        return fused(
            mesh,
            video_in,
            audio_in,
            q_self,
            k_self,
            v_self,
            q_a2v,
            k_a2v,
            v_a2v,
            q_v2a,
            k_v2a,
            v_v2a,
            wo_self,
            wo_a2v,
            wo_v2a,
            video_gates,
            audio_gates,
            video_steps,
            audio_steps,
            audio_len,
        )
    heads_self = q_self.shape[1] // DHV
    heads_cross = q_a2v.shape[1] // DHC
    rows_video = q_self.shape[0]
    rows_audio = q_v2a.shape[0]
    limit = audio_len[0]
    piece = (
        lax.all_gather(k_a2v, "seq", axis=0, tiled=True),
        lax.all_gather(v_a2v, "seq", axis=0, tiled=True),
    )
    a2v_state = update_state(
        start_state(rows_video, heads_cross, DHC),
        q_a2v,
        piece[0],
        piece[1],
        heads_cross,
        DHC,
        jnp.int32(0),
        limit,
    )
    a2v_att = finish(a2v_state, heads_cross, DHC)
    piece = (
        lax.all_gather(k_self, "seq", axis=0, tiled=True),
        lax.all_gather(v_self, "seq", axis=0, tiled=True),
    )
    self_state = update_state(
        start_state(rows_video, heads_self, DHV),
        q_self,
        piece[0],
        piece[1],
        heads_self,
        DHV,
        jnp.int32(0),
        None,
    )
    piece = (
        lax.all_gather(k_v2a, "seq", axis=0, tiled=True),
        lax.all_gather(v_v2a, "seq", axis=0, tiled=True),
    )
    v2a_state = update_state(
        start_state(rows_audio, heads_cross, DHC),
        q_v2a,
        piece[0],
        piece[1],
        heads_cross,
        DHC,
        jnp.int32(0),
        None,
    )
    self_att = finish(self_state, heads_self, DHV)
    v2a_att = finish(v2a_state, heads_cross, DHC)
    levels = jnp.arange(NT, dtype=jnp.int32)
    video_hot = (video_steps[:, None] == levels[None, :]).astype(jnp.bfloat16)
    video_gain = jnp.dot(video_hot, video_gates.reshape(NT, -1), preferred_element_type=jnp.float32)
    width_video = video_gates.shape[2]
    video_term = video_gain[:, :width_video] * jnp.dot(
        self_att, wo_self, preferred_element_type=jnp.float32
    )
    video_term = video_term + video_gain[:, width_video:] * jnp.dot(
        a2v_att, wo_a2v, preferred_element_type=jnp.float32
    )
    audio_hot = (audio_steps[:, None] == levels[None, :]).astype(jnp.bfloat16)
    audio_gain = jnp.dot(audio_hot, audio_gates, preferred_element_type=jnp.float32)
    positions = lax.axis_index("seq") * rows_audio + jnp.arange(rows_audio, dtype=jnp.int32)
    present = (positions < limit).astype(jnp.float32)
    audio_term = (
        present[:, None] * audio_gain * jnp.dot(v2a_att, wo_v2a, preferred_element_type=jnp.float32)
    )
    video_sum, audio_sum = (
        lax.psum_scatter(
            video_term.astype(jnp.bfloat16), ("mp", "sub"), scatter_dimension=1, tiled=True
        ).astype(jnp.float32),
        lax.psum_scatter(
            audio_term.astype(jnp.bfloat16), ("mp", "sub"), scatter_dimension=1, tiled=True
        ).astype(jnp.float32),
    )
    video_out = (video_in.astype(jnp.float32) + video_sum).astype(jnp.bfloat16)
    audio_out = (audio_in.astype(jnp.float32) + audio_sum).astype(jnp.bfloat16)
    return (video_out, audio_out)


def solution(mesh):
    in_specs = (
        P(("groups", "seq"), ("mp", "sub")),
        P(("groups", "seq"), ("mp", "sub")),
        P(("groups", "seq"), ("mp", "sub")),
        P(("groups", "seq"), ("mp", "sub")),
        P(("groups", "seq"), ("mp", "sub")),
        P(("groups", "seq"), ("mp", "sub")),
        P(("groups", "seq"), ("mp", "sub")),
        P(("groups", "seq"), ("mp", "sub")),
        P(("groups", "seq"), ("mp", "sub")),
        P(("groups", "seq"), ("mp", "sub")),
        P(("groups", "seq"), ("mp", "sub")),
        P(("mp", "sub"), None),
        P(("mp", "sub"), None),
        P(("mp", "sub"), None),
        P(),
        P(),
        P(("groups", "seq")),
        P(("groups", "seq")),
        P("groups"),
    )
    out_specs = (P(("groups", "seq"), ("mp", "sub")), P(("groups", "seq"), ("mp", "sub")))
    return jax.shard_map(
        functools.partial(on_device, mesh), mesh=mesh, in_specs=in_specs, out_specs=out_specs, check_vma=False
    )
```

```python
import functools
import math

import jax
import jax.numpy as jnp
from jax import lax
from jax.experimental import pallas as pl
from jax.experimental.pallas import tpu as pltpu
from jax.sharding import PartitionSpec as P

DHV = 128
DHC = 64
NT = 16


def start_state(rows, heads, width):
    return (
        jnp.full((rows, heads), -1e30, jnp.float32),
        jnp.zeros((rows, heads), jnp.float32),
        jnp.zeros((rows, heads, width), jnp.float32),
    )


def update_block(state, queries, keys, values, heads, width, allowed):
    rows = queries.shape[0]
    count = keys.shape[0]
    q_heads = queries.reshape(rows, heads, width)
    k_heads = keys.reshape(count, heads, width)
    v_heads = values.reshape(count, heads, width)
    scores = jnp.einsum(
        "qhd,khd->qhk", q_heads, k_heads, preferred_element_type=jnp.float32
    ) / math.sqrt(width)
    if allowed is not None:
        scores = jnp.where(allowed[None, None, :], scores, -jnp.inf)
    peak_old, total_old, summed_old = state
    peak = jnp.maximum(peak_old, jnp.max(scores, axis=2))
    weights = jnp.exp(scores - peak[:, :, None])
    factor = jnp.exp(peak_old - peak)
    total = total_old * factor + jnp.sum(weights, axis=2)
    summed = summed_old * factor[:, :, None] + jnp.einsum(
        "qhk,khd->qhd", weights.astype(jnp.bfloat16), v_heads, preferred_element_type=jnp.float32
    )
    return (peak, total, summed)


def update_state(state, queries, keys, values, heads, width, start, limit):
    count = keys.shape[0]
    block = 1024 if count > 1024 and count % 1024 == 0 else count
    if block == count:
        allowed = None
        if limit is not None:
            allowed = jnp.arange(count, dtype=jnp.int32) < limit
        return update_block(state, queries, keys, values, heads, width, allowed)
    steps = count // block
    key_blocks = keys.reshape(steps, block, keys.shape[1])
    value_blocks = values.reshape(steps, block, values.shape[1])
    offsets = jnp.arange(steps, dtype=jnp.int32) * block

    def one_block(carry, items):
        key_rows, value_rows, offset = items
        allowed = None
        if limit is not None:
            allowed = start + offset + jnp.arange(block, dtype=jnp.int32) < limit
        return (update_block(carry, queries, key_rows, value_rows, heads, width, allowed), None)

    result, _ = lax.scan(one_block, state, (key_blocks, value_blocks, offsets))
    return result


def finish(state, heads, width):
    peak, total, summed = state
    rows = summed.shape[0]
    return (summed / total[:, :, None]).reshape(rows, heads * width).astype(jnp.bfloat16)


MESH = pl.DeviceIdType.MESH
BF16 = jnp.bfloat16
F32 = jnp.float32
CHUNKS = 4


def fits(mesh, q_self, q_a2v, k_a2v):
    seq = mesh.shape["seq"]
    return (
        seq > 1
        and q_self.shape[1] == seq * DHV
        and q_a2v.shape[1] == seq * DHC
        and 2 * DHC == DHV
        and seq % 2 == 0
        and k_a2v.shape[0] % 32 == 0
        and seq * q_self.shape[0] <= 1024
        and mesh.shape["sub"] == 2
        and mesh.shape["mp"] > 1
    )


def attend(queries, keys, values, width, allowed=None):
    scores = lax.dot_general(
        queries, keys, (((1,), (1,)), ((), ())), preferred_element_type=F32
    )
    if allowed is not None:
        scores = jnp.where(allowed, scores, -jnp.inf)
    peak = jnp.max(scores, axis=1, keepdims=True)
    weights = jnp.exp2((scores - peak) * (math.log2(math.e) / math.sqrt(width)))
    total = jnp.sum(weights, axis=1, keepdims=True)
    summed = jnp.dot(weights.astype(BF16), values, preferred_element_type=F32)
    return summed / total


def spread(hot, table):
    return lax.dot_general(hot, table, (((0,), (0,)), ((), ())), preferred_element_type=F32)


def kernel(
    seq,
    mp,
    video_in,
    audio_in,
    q_self,
    k_self,
    v_self,
    q_a2v,
    k_a2v,
    v_a2v,
    q_v2a,
    k_v2a,
    v_v2a,
    wo_self,
    wo_a2v,
    wo_v2a,
    video_gates,
    audio_gates,
    video_steps,
    audio_steps,
    audio_len,
    video_out,
    audio_out,
    qs,
    ks,
    vs,
    qa,
    ka,
    va,
    qv_in,
    kv_in,
    vv_in,
    q_pack,
    kv_pack,
    q_got,
    kv_got,
    os_send,
    os,
    ov_send,
    ov_got,
    ws,
    wa,
    wv,
    vg,
    ag,
    vin,
    ain,
    vsteps,
    asteps,
    alen,
    vout,
    aout,
    gain,
    term,
    core_send,
    core_got,
    kept,
    mp_send,
    mp_got,
    acore_send,
    acore_got,
    akept,
    amp_send,
    amp_got,
    local_sem,
    seq_send_sem,
    seq_recv_sem,
    core_send_sem,
    core_recv_sem,
    mp_send_sem,
    mp_recv_sem,
):
    me = lax.axis_index("seq")
    my_mp = lax.axis_index("mp")
    my_sub = lax.axis_index("sub")
    rows = q_self.shape[0]
    arows = k_a2v.shape[0]
    width_v = wo_self.shape[1]
    width_a = wo_v2a.shape[1]
    owned_v = width_v // (2 * mp)
    owned_a = width_a // (2 * mp)
    part = owned_v // CHUNKS

    def at(index, size):
        return pl.ds(pl.multiple_of(index * size, size), size)

    def peer(d):
        return lax.rem(me + d, seq)

    def other_mp(d):
        return lax.rem(my_mp + d, mp)

    local = []

    def bring(source, target):
        copy = pltpu.make_async_copy(source, target, local_sem.at[len(local)])
        copy.start()
        local.append(copy)
        return copy

    cross = [
        bring(q_v2a, qv_in),
        bring(k_v2a, kv_in),
        bring(v_v2a, vv_in),
    ]
    first = [
        bring(video_steps, vsteps),
        bring(audio_len, alen),
        bring(video_gates, vg),
        bring(q_a2v, qa),
        bring(k_a2v, ka.at[at(me, arows)]),
        bring(v_a2v, va.at[at(me, arows)]),
        bring(wo_a2v, wa),
    ]
    own = [
        bring(q_self.at[:, at(me, DHV)], qs.at[at(me, rows)]),
        bring(k_self.at[:, at(me, DHV)], ks.at[at(me, rows)]),
        bring(v_self.at[:, at(me, DHV)], vs.at[at(me, rows)]),
    ]
    late = [
        bring(wo_self, ws),
        bring(wo_v2a, wv),
        bring(audio_gates, ag),
        bring(audio_steps, asteps),
        bring(video_in, vin),
        bring(audio_in, ain),
    ]

    barrier = pltpu.get_barrier_semaphore()
    for d in range(1, seq):
        pl.semaphore_signal(barrier, inc=1, device_id={"seq": peer(d)}, device_id_type=MESH)
    pl.semaphore_signal(barrier, inc=1, device_id={"sub": 1 - my_sub}, device_id_type=MESH)
    for d in range(1, mp):
        pl.semaphore_signal(barrier, inc=1, device_id={"mp": other_mp(d)}, device_id_type=MESH)
    pl.semaphore_wait(barrier, seq - 1 + 1 + mp - 1)

    sent = []

    def to_seq(kind, d, source, target):
        copy = pltpu.make_async_remote_copy(
            src_ref=source,
            dst_ref=target,
            send_sem=seq_send_sem.at[kind, d],
            recv_sem=seq_recv_sem.at[kind, d],
            device_id={"seq": peer(d)},
            device_id_type=MESH,
        )
        copy.start()
        sent.append(copy)
        return copy

    order = [d for d in range(1, seq)]
    self_in = []
    for kind, (source, target) in enumerate(((k_self, ks), (q_self, qs), (v_self, vs))):
        for d in order:
            self_in.append(
                to_seq(kind, d, source.at[:, at(peer(d), DHV)], target.at[at(me, rows)])
            )
    a2v_in = []
    for kind, (source, target) in enumerate(((k_a2v, ka), (v_a2v, va))):
        for d in order:
            a2v_in.append(to_seq(3 + kind, d, source, target.at[at(me, arows)]))

    for copy in cross:
        copy.wait()
    half = arows // 2
    for h in range(seq):
        cols = slice(h * DHC, (h + 1) * DHC)
        kv = jnp.concatenate(
            [kv_in[:, cols].astype(F32), vv_in[:, cols].astype(F32)], axis=1
        ).astype(BF16)
        qh = qv_in[:, cols].astype(F32)
        kv_pack[h] = kv
        q_pack[h] = jnp.concatenate([qh[:half], qh[half:]], axis=1).astype(BF16)
    v2a_in = []
    for d in order:
        v2a_in.append(to_seq(5, d, q_pack.at[peer(d)], q_got.at[me]))
        v2a_in.append(to_seq(6, d, kv_pack.at[peer(d)], kv_got.at[at(me, rows)]))
    q_got[me] = q_pack[me]
    kv_got[at(me, rows), :] = kv_pack[me]

    for copy in first:
        copy.wait()
    picks = lax.broadcasted_iota(jnp.int32, (vg.shape[0], rows), 0)
    hot = (picks == vsteps[...]).astype(F32).astype(BF16)
    tile = min(512, width_v)
    for c in range(width_v // tile):
        cols = slice(c * tile, (c + 1) * tile)
        gain[:, cols] = spread(hot, vg[:, 0, cols]).astype(BF16)
    for copy in a2v_in:
        copy.wait_recv()
    count = seq * arows
    limit = alen[0]
    allowed = lax.broadcasted_iota(jnp.int32, (2 * rows, count), 1) < limit
    low = lax.broadcasted_iota(jnp.int32, (rows, 2 * DHC), 1) < DHC
    pieces = []
    for pair in range(seq // 2):
        cols = slice(pair * 2 * DHC, (pair + 1) * 2 * DHC)
        qp = qa[:, cols]
        zero = jnp.zeros_like(qp)
        both = jnp.concatenate([jnp.where(low, qp, zero), jnp.where(low, zero, qp)], axis=0)
        out = attend(both, ka[:, cols], va[:, cols], DHC, allowed)
        pieces.append(jnp.where(low, out[:rows], out[rows:]).astype(BF16))
    a2v_att = jnp.concatenate(pieces, axis=1)
    for c in range(width_v // tile):
        cols = slice(c * tile, (c + 1) * tile)
        term[:, cols] = spread(hot, vg[:, 1, cols]) * jnp.dot(
            a2v_att, wa[:, cols], preferred_element_type=F32
        )

    for copy in own:
        copy.wait()
    for copy in self_in:
        copy.wait_recv()
    self_back = []
    for d in order + [0]:
        out = attend(qs[at(peer(d), rows), :], ks[...], vs[...], DHV).astype(BF16)
        if d == 0:
            os[:, at(me, DHV)] = out
        else:
            os_send[d] = out
            self_back.append(to_seq(7, d, os_send.at[d], os.at[:, at(me, DHV)]))

    for copy in v2a_in:
        copy.wait_recv()
    blocks = []
    for p in range(seq):
        got = q_got[p].astype(F32)
        blocks.append(got[:, :DHC])
        blocks.append(got[:, DHC:])
    qv = jnp.concatenate(blocks, axis=0)
    qv = jnp.concatenate([qv, jnp.zeros_like(qv)], axis=1).astype(BF16)
    out = attend(qv, kv_got[...], kv_got[...], DHC)[:, DHC:]
    for p in range(seq):
        top = out[p * arows : p * arows + half]
        bottom = out[p * arows + half : (p + 1) * arows]
        ov_send[p] = jnp.concatenate([top, bottom], axis=1).astype(BF16)
    v2a_back = []
    for d in order:
        v2a_back.append(to_seq(8, d, ov_send.at[peer(d)], ov_got.at[me]))
    ov_got[me] = ov_send[me]

    for copy in late:
        copy.wait()
    for copy in self_back:
        copy.wait_recv()
    self_att = os[...]

    def owner(m, s):
        return 2 * m + s

    def video_part(m, s, c):
        cols = pl.ds(pl.multiple_of(owner(m, s) * owned_v + c * part, part), part)
        return term[:, cols] + gain[:, cols].astype(F32) * jnp.dot(
            self_att, ws[:, cols], preferred_element_type=F32
        )

    def to_core(c, source, target):
        copy = pltpu.make_async_remote_copy(
            src_ref=source,
            dst_ref=target,
            send_sem=core_send_sem.at[c],
            recv_sem=core_recv_sem.at[c],
            device_id={"sub": 1 - my_sub},
            device_id_type=MESH,
        )
        copy.start()
        sent.append(copy)
        return copy

    def to_mp(c, d, source, target):
        copy = pltpu.make_async_remote_copy(
            src_ref=source,
            dst_ref=target,
            send_sem=mp_send_sem.at[c, d],
            recv_sem=mp_recv_sem.at[c, d],
            device_id={"mp": other_mp(d)},
            device_id_type=MESH,
        )
        copy.start()
        sent.append(copy)
        return copy

    core_copies = {}
    mp_copies = {}

    def pass_on(c):
        core_copies[c].wait_recv()
        for d in range(1, mp):
            mp_send[c, d] = (kept[c, d] + core_got[c, d].astype(F32)).astype(BF16)
            mp_copies[c, d] = to_mp(c, d, mp_send.at[c, d], mp_got.at[c, d])
        kept[c, 0] = kept[c, 0] + core_got[c, 0].astype(F32)

    for c in range(CHUNKS):
        for d in range(mp):
            core_send[c, d] = video_part(other_mp(d), 1 - my_sub, c).astype(BF16)
        core_copies[c] = to_core(c, core_send.at[c], core_got.at[c])
        for d in range(mp):
            kept[c, d] = video_part(other_mp(d), my_sub, c)
        if c > 0:
            pass_on(c - 1)
    pass_on(CHUNKS - 1)

    for copy in v2a_back:
        copy.wait_recv()
    blocks = []
    for h in range(seq):
        got = ov_got[h].astype(F32)
        blocks.append(jnp.concatenate([got[:, :DHC], got[:, DHC:]], axis=0))
    v2a_att = jnp.concatenate(blocks, axis=1).astype(BF16)
    apicks = lax.broadcasted_iota(jnp.int32, (ag.shape[0], arows), 0)
    hot_audio = (apicks == asteps[...]).astype(F32).astype(BF16)
    positions = me * arows + lax.broadcasted_iota(jnp.int32, (arows, owned_a), 0)
    present = (positions < limit).astype(F32)

    def audio_part(m, s):
        cols = at(owner(m, s), owned_a)
        return (
            present
            * spread(hot_audio, ag[:, cols])
            * jnp.dot(v2a_att, wv[:, cols], preferred_element_type=F32)
        )

    for d in range(mp):
        acore_send[d] = audio_part(other_mp(d), 1 - my_sub).astype(BF16)
    acore = to_core(CHUNKS, acore_send, acore_got)
    for d in range(mp):
        akept[d] = audio_part(other_mp(d), my_sub)
    acore.wait_recv()
    for d in range(1, mp):
        amp_send[d] = (akept[d] + acore_got[d].astype(F32)).astype(BF16)
        mp_copies[CHUNKS, d] = to_mp(CHUNKS, d, amp_send.at[d], amp_got.at[d])

    results = []
    for c in range(CHUNKS):
        cols = slice(c * part, (c + 1) * part)
        total = kept[c, 0]
        for d in range(1, mp):
            mp_copies[c, d].wait_recv()
            total = total + mp_got[c, d].astype(F32)
        vout[:, cols] = (vin[:, cols].astype(F32) + total).astype(BF16)
        results.append(bring(vout.at[:, cols], video_out.at[:, cols]))
    total = akept[0] + acore_got[0].astype(F32)
    for d in range(1, mp):
        mp_copies[CHUNKS, d].wait_recv()
        total = total + amp_got[d].astype(F32)
    aout[...] = (ain[...].astype(F32) + total).astype(BF16)
    results.append(bring(aout, audio_out))
    for copy in results:
        copy.wait()
    for copy in sent:
        copy.wait_send()


def fused(mesh, *args):
    (
        video_in,
        audio_in,
        q_self,
        _,
        _,
        q_a2v,
        k_a2v,
        _,
        q_v2a,
        k_v2a,
        _,
        wo_self,
        wo_a2v,
        wo_v2a,
        video_gates,
        audio_gates,
        video_steps,
        audio_steps,
        _,
    ) = args
    seq, mp = mesh.shape["seq"], mesh.shape["mp"]
    rows, arows = q_self.shape[0], k_a2v.shape[0]
    args = list(args)
    args[16] = video_steps.reshape(1, rows)
    args[17] = audio_steps.reshape(1, arows)
    part = video_in.shape[1] // CHUNKS
    owned_a = audio_in.shape[1]

    def buffer(*shape, dtype=BF16):
        return pltpu.VMEM(shape, dtype)

    like = lambda array: pltpu.VMEM(array.shape, array.dtype)
    scratch = [
        buffer(seq * rows, DHV),
        buffer(seq * rows, DHV),
        buffer(seq * rows, DHV),
        like(q_a2v),
        buffer(seq * arows, seq * DHC),
        buffer(seq * arows, seq * DHC),
        like(q_v2a),
        like(k_v2a),
        like(k_v2a),
        buffer(seq, arows // 2, 2 * DHC),
        buffer(seq, rows, 2 * DHC),
        buffer(seq, arows // 2, 2 * DHC),
        buffer(seq * rows, 2 * DHC),
        buffer(seq, rows, DHV),
        buffer(rows, seq * DHV),
        buffer(seq, arows // 2, 2 * DHC),
        buffer(seq, arows // 2, 2 * DHC),
        like(wo_self),
        like(wo_a2v),
        like(wo_v2a),
        like(video_gates),
        like(audio_gates),
        like(video_in),
        like(audio_in),
        buffer(1, rows, dtype=jnp.int32),
        buffer(1, arows, dtype=jnp.int32),
        pltpu.SMEM((1,), jnp.int32),
        like(video_in),
        like(audio_in),
        buffer(rows, wo_self.shape[1]),
        buffer(rows, wo_self.shape[1], dtype=F32),
        buffer(CHUNKS, mp, rows, part),
        buffer(CHUNKS, mp, rows, part),
        buffer(CHUNKS, mp, rows, part, dtype=F32),
        buffer(CHUNKS, mp, rows, part),
        buffer(CHUNKS, mp, rows, part),
        buffer(mp, arows, owned_a),
        buffer(mp, arows, owned_a),
        buffer(mp, arows, owned_a, dtype=F32),
        buffer(mp, arows, owned_a),
        buffer(mp, arows, owned_a),
        pltpu.SemaphoreType.DMA((32,)),
        pltpu.SemaphoreType.DMA((9, seq)),
        pltpu.SemaphoreType.DMA((9, seq)),
        pltpu.SemaphoreType.DMA((CHUNKS + 1,)),
        pltpu.SemaphoreType.DMA((CHUNKS + 1,)),
        pltpu.SemaphoreType.DMA((CHUNKS + 1, mp)),
        pltpu.SemaphoreType.DMA((CHUNKS + 1, mp)),
    ]
    anywhere = pl.BlockSpec(memory_space=pltpu.HBM)
    return pl.pallas_call(
        functools.partial(kernel, seq, mp),
        out_shape=(
            jax.ShapeDtypeStruct(video_in.shape, video_in.dtype),
            jax.ShapeDtypeStruct(audio_in.shape, audio_in.dtype),
        ),
        in_specs=[anywhere] * len(args),
        out_specs=(anywhere, anywhere),
        scratch_shapes=scratch,
        compiler_params=pltpu.CompilerParams(
            collective_id=0, has_side_effects=True, vmem_limit_bytes=63 * 1024 * 1024
        ),
    )(*args)


def on_device(
    mesh,
    video_in,
    audio_in,
    q_self,
    k_self,
    v_self,
    q_a2v,
    k_a2v,
    v_a2v,
    q_v2a,
    k_v2a,
    v_v2a,
    wo_self,
    wo_a2v,
    wo_v2a,
    video_gates,
    audio_gates,
    video_steps,
    audio_steps,
    audio_len,
):
    if fits(mesh, q_self, q_a2v, k_a2v):
        return fused(
            mesh,
            video_in,
            audio_in,
            q_self,
            k_self,
            v_self,
            q_a2v,
            k_a2v,
            v_a2v,
            q_v2a,
            k_v2a,
            v_v2a,
            wo_self,
            wo_a2v,
            wo_v2a,
            video_gates,
            audio_gates,
            video_steps,
            audio_steps,
            audio_len,
        )
    heads_self = q_self.shape[1] // DHV
    heads_cross = q_a2v.shape[1] // DHC
    rows_video = q_self.shape[0]
    rows_audio = q_v2a.shape[0]
    limit = audio_len[0]
    piece = (
        lax.all_gather(k_a2v, "seq", axis=0, tiled=True),
        lax.all_gather(v_a2v, "seq", axis=0, tiled=True),
    )
    a2v_state = update_state(
        start_state(rows_video, heads_cross, DHC),
        q_a2v,
        piece[0],
        piece[1],
        heads_cross,
        DHC,
        jnp.int32(0),
        limit,
    )
    a2v_att = finish(a2v_state, heads_cross, DHC)
    piece = (
        lax.all_gather(k_self, "seq", axis=0, tiled=True),
        lax.all_gather(v_self, "seq", axis=0, tiled=True),
    )
    self_state = update_state(
        start_state(rows_video, heads_self, DHV),
        q_self,
        piece[0],
        piece[1],
        heads_self,
        DHV,
        jnp.int32(0),
        None,
    )
    piece = (
        lax.all_gather(k_v2a, "seq", axis=0, tiled=True),
        lax.all_gather(v_v2a, "seq", axis=0, tiled=True),
    )
    v2a_state = update_state(
        start_state(rows_audio, heads_cross, DHC),
        q_v2a,
        piece[0],
        piece[1],
        heads_cross,
        DHC,
        jnp.int32(0),
        None,
    )
    self_att = finish(self_state, heads_self, DHV)
    v2a_att = finish(v2a_state, heads_cross, DHC)
    levels = jnp.arange(NT, dtype=jnp.int32)
    video_hot = (video_steps[:, None] == levels[None, :]).astype(jnp.bfloat16)
    video_gain = jnp.dot(video_hot, video_gates.reshape(NT, -1), preferred_element_type=jnp.float32)
    width_video = video_gates.shape[2]
    video_term = video_gain[:, :width_video] * jnp.dot(
        self_att, wo_self, preferred_element_type=jnp.float32
    )
    video_term = video_term + video_gain[:, width_video:] * jnp.dot(
        a2v_att, wo_a2v, preferred_element_type=jnp.float32
    )
    audio_hot = (audio_steps[:, None] == levels[None, :]).astype(jnp.bfloat16)
    audio_gain = jnp.dot(audio_hot, audio_gates, preferred_element_type=jnp.float32)
    positions = lax.axis_index("seq") * rows_audio + jnp.arange(rows_audio, dtype=jnp.int32)
    present = (positions < limit).astype(jnp.float32)
    audio_term = (
        present[:, None] * audio_gain * jnp.dot(v2a_att, wo_v2a, preferred_element_type=jnp.float32)
    )
    video_sum, audio_sum = (
        lax.psum_scatter(
            video_term.astype(jnp.bfloat16), ("mp", "sub"), scatter_dimension=1, tiled=True
        ).astype(jnp.float32),
        lax.psum_scatter(
            audio_term.astype(jnp.bfloat16), ("mp", "sub"), scatter_dimension=1, tiled=True
        ).astype(jnp.float32),
    )
    video_out = (video_in.astype(jnp.float32) + video_sum).astype(jnp.bfloat16)
    audio_out = (audio_in.astype(jnp.float32) + audio_sum).astype(jnp.bfloat16)
    return (video_out, audio_out)


def solution(mesh):
    in_specs = (
        P(("groups", "seq"), ("mp", "sub")),
        P(("groups", "seq"), ("mp", "sub")),
        P(("groups", "seq"), ("mp", "sub")),
        P(("groups", "seq"), ("mp", "sub")),
        P(("groups", "seq"), ("mp", "sub")),
        P(("groups", "seq"), ("mp", "sub")),
        P(("groups", "seq"), ("mp", "sub")),
        P(("groups", "seq"), ("mp", "sub")),
        P(("groups", "seq"), ("mp", "sub")),
        P(("groups", "seq"), ("mp", "sub")),
        P(("groups", "seq"), ("mp", "sub")),
        P(("mp", "sub"), None),
        P(("mp", "sub"), None),
        P(("mp", "sub"), None),
        P(),
        P(),
        P(("groups", "seq")),
        P(("groups", "seq")),
        P("groups"),
    )
    out_specs = (P(("groups", "seq"), ("mp", "sub")), P(("groups", "seq"), ("mp", "sub")))
    return jax.shard_map(
        functools.partial(on_device, mesh), mesh=mesh, in_specs=in_specs, out_specs=out_specs, check_vma=False
    )
```

```python
import functools
import math

import jax
import jax.numpy as jnp
from jax import lax
from jax.experimental import pallas as pl
from jax.experimental.pallas import tpu as pltpu
from jax.sharding import PartitionSpec as P

DHV = 128
DHC = 64
NT = 16


def start_state(rows, heads, width):
    return (
        jnp.full((rows, heads), -1e30, jnp.float32),
        jnp.zeros((rows, heads), jnp.float32),
        jnp.zeros((rows, heads, width), jnp.float32),
    )


def update_block(state, queries, keys, values, heads, width, allowed):
    rows = queries.shape[0]
    count = keys.shape[0]
    q_heads = queries.reshape(rows, heads, width)
    k_heads = keys.reshape(count, heads, width)
    v_heads = values.reshape(count, heads, width)
    scores = jnp.einsum(
        "qhd,khd->qhk", q_heads, k_heads, preferred_element_type=jnp.float32
    ) / math.sqrt(width)
    if allowed is not None:
        scores = jnp.where(allowed[None, None, :], scores, -jnp.inf)
    peak_old, total_old, summed_old = state
    peak = jnp.maximum(peak_old, jnp.max(scores, axis=2))
    weights = jnp.exp(scores - peak[:, :, None])
    factor = jnp.exp(peak_old - peak)
    total = total_old * factor + jnp.sum(weights, axis=2)
    summed = summed_old * factor[:, :, None] + jnp.einsum(
        "qhk,khd->qhd", weights.astype(jnp.bfloat16), v_heads, preferred_element_type=jnp.float32
    )
    return (peak, total, summed)


def update_state(state, queries, keys, values, heads, width, start, limit):
    count = keys.shape[0]
    block = 1024 if count > 1024 and count % 1024 == 0 else count
    if block == count:
        allowed = None
        if limit is not None:
            allowed = jnp.arange(count, dtype=jnp.int32) < limit
        return update_block(state, queries, keys, values, heads, width, allowed)
    steps = count // block
    key_blocks = keys.reshape(steps, block, keys.shape[1])
    value_blocks = values.reshape(steps, block, values.shape[1])
    offsets = jnp.arange(steps, dtype=jnp.int32) * block

    def one_block(carry, items):
        key_rows, value_rows, offset = items
        allowed = None
        if limit is not None:
            allowed = start + offset + jnp.arange(block, dtype=jnp.int32) < limit
        return (update_block(carry, queries, key_rows, value_rows, heads, width, allowed), None)

    result, _ = lax.scan(one_block, state, (key_blocks, value_blocks, offsets))
    return result


def finish(state, heads, width):
    peak, total, summed = state
    rows = summed.shape[0]
    return (summed / total[:, :, None]).reshape(rows, heads * width).astype(jnp.bfloat16)


MESH = pl.DeviceIdType.MESH
BF16 = jnp.bfloat16
F32 = jnp.float32
CHUNKS = 2


def fits(mesh, q_self, q_a2v, k_a2v):
    seq = mesh.shape["seq"]
    return (
        seq > 1
        and q_self.shape[1] == seq * DHV
        and q_a2v.shape[1] == seq * DHC
        and 2 * DHC == DHV
        and seq % 2 == 0
        and k_a2v.shape[0] % 32 == 0
        and seq * q_self.shape[0] <= 1024
        and mesh.shape["sub"] == 2
        and mesh.shape["mp"] > 1
    )


def attend(queries, keys, values, width, allowed=None):
    scores = lax.dot_general(
        queries, keys, (((1,), (1,)), ((), ())), preferred_element_type=F32
    )
    if allowed is not None:
        scores = jnp.where(allowed, scores, -jnp.inf)
    peak = jnp.max(scores, axis=1, keepdims=True)
    weights = jnp.exp2((scores - peak) * (math.log2(math.e) / math.sqrt(width)))
    total = jnp.sum(weights, axis=1, keepdims=True)
    summed = jnp.dot(weights.astype(BF16), values, preferred_element_type=F32)
    return summed / total


def spread(hot, table):
    return lax.dot_general(hot, table, (((0,), (0,)), ((), ())), preferred_element_type=F32)


def kernel(
    seq,
    mp,
    video_in,
    audio_in,
    q_self,
    k_self,
    v_self,
    q_a2v,
    k_a2v,
    v_a2v,
    q_v2a,
    k_v2a,
    v_v2a,
    wo_self,
    wo_a2v,
    wo_v2a,
    video_gates,
    audio_gates,
    video_steps,
    audio_steps,
    audio_len,
    video_out,
    audio_out,
    qs,
    ks,
    vs,
    qa,
    ka,
    va,
    qv_in,
    kv_in,
    vv_in,
    q_pack,
    kv_pack,
    q_got,
    kv_got,
    os_send,
    os,
    ov_send,
    ov_got,
    ws,
    wa,
    wv,
    vg,
    ag,
    vin,
    ain,
    vsteps,
    asteps,
    alen,
    vout,
    aout,
    gain,
    term,
    core_send,
    core_got,
    kept,
    mp_send,
    mp_got,
    acore_send,
    acore_got,
    akept,
    amp_send,
    amp_got,
    local_sem,
    seq_send_sem,
    seq_recv_sem,
    core_send_sem,
    core_recv_sem,
    mp_send_sem,
    mp_recv_sem,
):
    me = lax.axis_index("seq")
    my_mp = lax.axis_index("mp")
    my_sub = lax.axis_index("sub")
    rows = q_self.shape[0]
    arows = k_a2v.shape[0]
    width_v = wo_self.shape[1]
    width_a = wo_v2a.shape[1]
    owned_v = width_v // (2 * mp)
    owned_a = width_a // (2 * mp)
    part = owned_v // CHUNKS

    def at(index, size):
        return pl.ds(pl.multiple_of(index * size, size), size)

    def peer(d):
        return lax.rem(me + d, seq)

    def other_mp(d):
        return lax.rem(my_mp + d, mp)

    local = []

    def bring(source, target):
        copy = pltpu.make_async_copy(source, target, local_sem.at[len(local)])
        copy.start()
        local.append(copy)
        return copy

    cross = [
        bring(q_v2a, qv_in),
        bring(k_v2a, kv_in),
        bring(v_v2a, vv_in),
    ]
    first = [
        bring(video_steps, vsteps),
        bring(audio_len, alen),
        bring(video_gates, vg),
        bring(q_a2v, qa),
        bring(k_a2v, ka.at[at(me, arows)]),
        bring(v_a2v, va.at[at(me, arows)]),
        bring(wo_a2v, wa),
    ]
    own = [
        bring(q_self.at[:, at(me, DHV)], qs.at[at(me, rows)]),
        bring(k_self.at[:, at(me, DHV)], ks.at[at(me, rows)]),
        bring(v_self.at[:, at(me, DHV)], vs.at[at(me, rows)]),
    ]
    late = [
        bring(wo_self, ws),
        bring(wo_v2a, wv),
        bring(audio_gates, ag),
        bring(audio_steps, asteps),
        bring(video_in, vin),
        bring(audio_in, ain),
    ]

    barrier = pltpu.get_barrier_semaphore()
    for d in range(1, seq):
        pl.semaphore_signal(barrier, inc=1, device_id={"seq": peer(d)}, device_id_type=MESH)
    pl.semaphore_signal(barrier, inc=1, device_id={"sub": 1 - my_sub}, device_id_type=MESH)
    for d in range(1, mp):
        pl.semaphore_signal(barrier, inc=1, device_id={"mp": other_mp(d)}, device_id_type=MESH)
    pl.semaphore_wait(barrier, seq - 1 + 1 + mp - 1)

    sent = []

    def to_seq(kind, d, source, target):
        copy = pltpu.make_async_remote_copy(
            src_ref=source,
            dst_ref=target,
            send_sem=seq_send_sem.at[kind, d],
            recv_sem=seq_recv_sem.at[kind, d],
            device_id={"seq": peer(d)},
            device_id_type=MESH,
        )
        copy.start()
        sent.append(copy)
        return copy

    order = [d for d in range(1, seq)]
    self_in = []
    for kind, (source, target) in enumerate(((k_self, ks), (q_self, qs), (v_self, vs))):
        for d in order:
            self_in.append(
                to_seq(kind, d, source.at[:, at(peer(d), DHV)], target.at[at(me, rows)])
            )
    a2v_in = []
    for kind, (source, target) in enumerate(((k_a2v, ka), (v_a2v, va))):
        for d in order:
            a2v_in.append(to_seq(3 + kind, d, source, target.at[at(me, arows)]))

    for copy in cross:
        copy.wait()
    half = arows // 2
    for h in range(seq):
        cols = slice(h * DHC, (h + 1) * DHC)
        kv = jnp.concatenate(
            [kv_in[:, cols].astype(F32), vv_in[:, cols].astype(F32)], axis=1
        ).astype(BF16)
        qh = qv_in[:, cols].astype(F32)
        kv_pack[h] = kv
        q_pack[h] = jnp.concatenate([qh[:half], qh[half:]], axis=1).astype(BF16)
    q_got[me] = q_pack[me]
    kv_got[at(me, rows), :] = kv_pack[me]

    for copy in first:
        copy.wait()
    picks = lax.broadcasted_iota(jnp.int32, (vg.shape[0], rows), 0)
    hot = (picks == vsteps[...]).astype(F32).astype(BF16)
    tile = min(512, width_v)
    for c in range(width_v // tile):
        cols = slice(c * tile, (c + 1) * tile)
        gain[:, cols] = spread(hot, vg[:, 0, cols]).astype(BF16)
    for copy in own:
        copy.wait()
    for copy in self_in:
        copy.wait_recv()
    self_back = []
    for d in order + [0]:
        out = attend(qs[at(peer(d), rows), :], ks[...], vs[...], DHV).astype(BF16)
        if d == 0:
            os[:, at(me, DHV)] = out
        else:
            os_send[d] = out
            self_back.append(to_seq(7, d, os_send.at[d], os.at[:, at(me, DHV)]))

    v2a_in = []
    for d in order:
        v2a_in.append(to_seq(5, d, q_pack.at[peer(d)], q_got.at[me]))
        v2a_in.append(to_seq(6, d, kv_pack.at[peer(d)], kv_got.at[at(me, rows)]))

    for copy in a2v_in:
        copy.wait_recv()
    count = seq * arows
    limit = alen[0]
    allowed = lax.broadcasted_iota(jnp.int32, (2 * rows, count), 1) < limit
    low = lax.broadcasted_iota(jnp.int32, (rows, 2 * DHC), 1) < DHC
    pieces = []
    for pair in range(seq // 2):
        cols = slice(pair * 2 * DHC, (pair + 1) * 2 * DHC)
        qp = qa[:, cols]
        zero = jnp.zeros_like(qp)
        both = jnp.concatenate([jnp.where(low, qp, zero), jnp.where(low, zero, qp)], axis=0)
        out = attend(both, ka[:, cols], va[:, cols], DHC, allowed)
        pieces.append(jnp.where(low, out[:rows], out[rows:]).astype(BF16))
    a2v_att = jnp.concatenate(pieces, axis=1)
    for c in range(width_v // tile):
        cols = slice(c * tile, (c + 1) * tile)
        term[:, cols] = spread(hot, vg[:, 1, cols]) * jnp.dot(
            a2v_att, wa[:, cols], preferred_element_type=F32
        )

    for copy in late:
        copy.wait()
    for copy in self_back:
        copy.wait_recv()
    self_att = os[...]

    def owner(m, s):
        return 2 * m + s

    def video_part(m, s, c):
        cols = pl.ds(pl.multiple_of(owner(m, s) * owned_v + c * part, part), part)
        return term[:, cols] + gain[:, cols].astype(F32) * jnp.dot(
            self_att, ws[:, cols], preferred_element_type=F32
        )

    def to_core(c, d, source, target):
        copy = pltpu.make_async_remote_copy(
            src_ref=source,
            dst_ref=target,
            send_sem=core_send_sem.at[c, d],
            recv_sem=core_recv_sem.at[c, d],
            device_id={"sub": 1 - my_sub},
            device_id_type=MESH,
        )
        copy.start()
        sent.append(copy)
        return copy

    def to_mp(c, d, source, target):
        copy = pltpu.make_async_remote_copy(
            src_ref=source,
            dst_ref=target,
            send_sem=mp_send_sem.at[c, d],
            recv_sem=mp_recv_sem.at[c, d],
            device_id={"mp": other_mp(d)},
            device_id_type=MESH,
        )
        copy.start()
        sent.append(copy)
        return copy

    core_copies = {}
    mp_copies = {}

    def exchange(c, d):
        core_send[c, d] = video_part(other_mp(d), 1 - my_sub, c).astype(BF16)
        core_copies[c, d] = to_core(c, d, core_send.at[c, d], core_got.at[c, d])
        kept[c, d] = video_part(other_mp(d), my_sub, c)

    def pass_on(c):
        for d in range(1, mp):
            core_copies[c, d].wait_recv()
            mp_send[c, d] = (kept[c, d] + core_got[c, d].astype(F32)).astype(BF16)
            mp_copies[c, d] = to_mp(c, d, mp_send.at[c, d], mp_got.at[c, d])

    for c in range(CHUNKS):
        for d in range(1, mp):
            exchange(c, d)
        if c > 0:
            pass_on(c - 1)
    pass_on(CHUNKS - 1)

    for copy in v2a_in:
        copy.wait_recv()
    blocks = []
    for p in range(seq):
        got = q_got[p].astype(F32)
        blocks.append(got[:, :DHC])
        blocks.append(got[:, DHC:])
    qv = jnp.concatenate(blocks, axis=0)
    qv = jnp.concatenate([qv, jnp.zeros_like(qv)], axis=1).astype(BF16)
    out = attend(qv, kv_got[...], kv_got[...], DHC)[:, DHC:]
    for p in range(seq):
        top = out[p * arows : p * arows + half]
        bottom = out[p * arows + half : (p + 1) * arows]
        ov_send[p] = jnp.concatenate([top, bottom], axis=1).astype(BF16)
    v2a_back = []
    for d in order:
        v2a_back.append(to_seq(8, d, ov_send.at[peer(d)], ov_got.at[me]))
    ov_got[me] = ov_send[me]

    for c in range(CHUNKS):
        exchange(c, 0)

    for copy in v2a_back:
        copy.wait_recv()
    blocks = []
    for h in range(seq):
        got = ov_got[h].astype(F32)
        blocks.append(jnp.concatenate([got[:, :DHC], got[:, DHC:]], axis=0))
    v2a_att = jnp.concatenate(blocks, axis=1).astype(BF16)
    apicks = lax.broadcasted_iota(jnp.int32, (ag.shape[0], arows), 0)
    hot_audio = (apicks == asteps[...]).astype(F32).astype(BF16)
    positions = me * arows + lax.broadcasted_iota(jnp.int32, (arows, owned_a), 0)
    present = (positions < limit).astype(F32)

    def audio_part(m, s):
        cols = at(owner(m, s), owned_a)
        return (
            present
            * spread(hot_audio, ag[:, cols])
            * jnp.dot(v2a_att, wv[:, cols], preferred_element_type=F32)
        )

    for d in range(mp):
        acore_send[d] = audio_part(other_mp(d), 1 - my_sub).astype(BF16)
    acore = to_core(CHUNKS, 0, acore_send, acore_got)
    for d in range(mp):
        akept[d] = audio_part(other_mp(d), my_sub)
    acore.wait_recv()
    for d in range(1, mp):
        amp_send[d] = (akept[d] + acore_got[d].astype(F32)).astype(BF16)
        mp_copies[CHUNKS, d] = to_mp(CHUNKS, d, amp_send.at[d], amp_got.at[d])

    results = []
    for c in range(CHUNKS):
        cols = slice(c * part, (c + 1) * part)
        core_copies[c, 0].wait_recv()
        total = kept[c, 0] + core_got[c, 0].astype(F32)
        for d in range(1, mp):
            mp_copies[c, d].wait_recv()
            total = total + mp_got[c, d].astype(F32)
        vout[:, cols] = (vin[:, cols].astype(F32) + total).astype(BF16)
        results.append(bring(vout.at[:, cols], video_out.at[:, cols]))
    total = akept[0] + acore_got[0].astype(F32)
    for d in range(1, mp):
        mp_copies[CHUNKS, d].wait_recv()
        total = total + amp_got[d].astype(F32)
    aout[...] = (ain[...].astype(F32) + total).astype(BF16)
    results.append(bring(aout, audio_out))
    for copy in results:
        copy.wait()
    for copy in sent:
        copy.wait_send()


def fused(mesh, *args):
    (
        video_in,
        audio_in,
        q_self,
        _,
        _,
        q_a2v,
        k_a2v,
        _,
        q_v2a,
        k_v2a,
        _,
        wo_self,
        wo_a2v,
        wo_v2a,
        video_gates,
        audio_gates,
        video_steps,
        audio_steps,
        _,
    ) = args
    seq, mp = mesh.shape["seq"], mesh.shape["mp"]
    rows, arows = q_self.shape[0], k_a2v.shape[0]
    args = list(args)
    args[16] = video_steps.reshape(1, rows)
    args[17] = audio_steps.reshape(1, arows)
    part = video_in.shape[1] // CHUNKS
    owned_a = audio_in.shape[1]

    def buffer(*shape, dtype=BF16):
        return pltpu.VMEM(shape, dtype)

    like = lambda array: pltpu.VMEM(array.shape, array.dtype)
    scratch = [
        buffer(seq * rows, DHV),
        buffer(seq * rows, DHV),
        buffer(seq * rows, DHV),
        like(q_a2v),
        buffer(seq * arows, seq * DHC),
        buffer(seq * arows, seq * DHC),
        like(q_v2a),
        like(k_v2a),
        like(k_v2a),
        buffer(seq, arows // 2, 2 * DHC),
        buffer(seq, rows, 2 * DHC),
        buffer(seq, arows // 2, 2 * DHC),
        buffer(seq * rows, 2 * DHC),
        buffer(seq, rows, DHV),
        buffer(rows, seq * DHV),
        buffer(seq, arows // 2, 2 * DHC),
        buffer(seq, arows // 2, 2 * DHC),
        like(wo_self),
        like(wo_a2v),
        like(wo_v2a),
        like(video_gates),
        like(audio_gates),
        like(video_in),
        like(audio_in),
        buffer(1, rows, dtype=jnp.int32),
        buffer(1, arows, dtype=jnp.int32),
        pltpu.SMEM((1,), jnp.int32),
        like(video_in),
        like(audio_in),
        buffer(rows, wo_self.shape[1]),
        buffer(rows, wo_self.shape[1], dtype=F32),
        buffer(CHUNKS, mp, rows, part),
        buffer(CHUNKS, mp, rows, part),
        buffer(CHUNKS, mp, rows, part, dtype=F32),
        buffer(CHUNKS, mp, rows, part),
        buffer(CHUNKS, mp, rows, part),
        buffer(mp, arows, owned_a),
        buffer(mp, arows, owned_a),
        buffer(mp, arows, owned_a, dtype=F32),
        buffer(mp, arows, owned_a),
        buffer(mp, arows, owned_a),
        pltpu.SemaphoreType.DMA((32,)),
        pltpu.SemaphoreType.DMA((9, seq)),
        pltpu.SemaphoreType.DMA((9, seq)),
        pltpu.SemaphoreType.DMA((CHUNKS + 1, mp)),
        pltpu.SemaphoreType.DMA((CHUNKS + 1, mp)),
        pltpu.SemaphoreType.DMA((CHUNKS + 1, mp)),
        pltpu.SemaphoreType.DMA((CHUNKS + 1, mp)),
    ]
    anywhere = pl.BlockSpec(memory_space=pltpu.HBM)
    return pl.pallas_call(
        functools.partial(kernel, seq, mp),
        out_shape=(
            jax.ShapeDtypeStruct(video_in.shape, video_in.dtype),
            jax.ShapeDtypeStruct(audio_in.shape, audio_in.dtype),
        ),
        in_specs=[anywhere] * len(args),
        out_specs=(anywhere, anywhere),
        scratch_shapes=scratch,
        compiler_params=pltpu.CompilerParams(
            collective_id=0, has_side_effects=True, vmem_limit_bytes=63 * 1024 * 1024
        ),
    )(*args)


def on_device(
    mesh,
    video_in,
    audio_in,
    q_self,
    k_self,
    v_self,
    q_a2v,
    k_a2v,
    v_a2v,
    q_v2a,
    k_v2a,
    v_v2a,
    wo_self,
    wo_a2v,
    wo_v2a,
    video_gates,
    audio_gates,
    video_steps,
    audio_steps,
    audio_len,
):
    if fits(mesh, q_self, q_a2v, k_a2v):
        return fused(
            mesh,
            video_in,
            audio_in,
            q_self,
            k_self,
            v_self,
            q_a2v,
            k_a2v,
            v_a2v,
            q_v2a,
            k_v2a,
            v_v2a,
            wo_self,
            wo_a2v,
            wo_v2a,
            video_gates,
            audio_gates,
            video_steps,
            audio_steps,
            audio_len,
        )
    heads_self = q_self.shape[1] // DHV
    heads_cross = q_a2v.shape[1] // DHC
    rows_video = q_self.shape[0]
    rows_audio = q_v2a.shape[0]
    limit = audio_len[0]
    piece = (
        lax.all_gather(k_a2v, "seq", axis=0, tiled=True),
        lax.all_gather(v_a2v, "seq", axis=0, tiled=True),
    )
    a2v_state = update_state(
        start_state(rows_video, heads_cross, DHC),
        q_a2v,
        piece[0],
        piece[1],
        heads_cross,
        DHC,
        jnp.int32(0),
        limit,
    )
    a2v_att = finish(a2v_state, heads_cross, DHC)
    piece = (
        lax.all_gather(k_self, "seq", axis=0, tiled=True),
        lax.all_gather(v_self, "seq", axis=0, tiled=True),
    )
    self_state = update_state(
        start_state(rows_video, heads_self, DHV),
        q_self,
        piece[0],
        piece[1],
        heads_self,
        DHV,
        jnp.int32(0),
        None,
    )
    piece = (
        lax.all_gather(k_v2a, "seq", axis=0, tiled=True),
        lax.all_gather(v_v2a, "seq", axis=0, tiled=True),
    )
    v2a_state = update_state(
        start_state(rows_audio, heads_cross, DHC),
        q_v2a,
        piece[0],
        piece[1],
        heads_cross,
        DHC,
        jnp.int32(0),
        None,
    )
    self_att = finish(self_state, heads_self, DHV)
    v2a_att = finish(v2a_state, heads_cross, DHC)
    levels = jnp.arange(NT, dtype=jnp.int32)
    video_hot = (video_steps[:, None] == levels[None, :]).astype(jnp.bfloat16)
    video_gain = jnp.dot(video_hot, video_gates.reshape(NT, -1), preferred_element_type=jnp.float32)
    width_video = video_gates.shape[2]
    video_term = video_gain[:, :width_video] * jnp.dot(
        self_att, wo_self, preferred_element_type=jnp.float32
    )
    video_term = video_term + video_gain[:, width_video:] * jnp.dot(
        a2v_att, wo_a2v, preferred_element_type=jnp.float32
    )
    audio_hot = (audio_steps[:, None] == levels[None, :]).astype(jnp.bfloat16)
    audio_gain = jnp.dot(audio_hot, audio_gates, preferred_element_type=jnp.float32)
    positions = lax.axis_index("seq") * rows_audio + jnp.arange(rows_audio, dtype=jnp.int32)
    present = (positions < limit).astype(jnp.float32)
    audio_term = (
        present[:, None] * audio_gain * jnp.dot(v2a_att, wo_v2a, preferred_element_type=jnp.float32)
    )
    video_sum, audio_sum = (
        lax.psum_scatter(
            video_term.astype(jnp.bfloat16), ("mp", "sub"), scatter_dimension=1, tiled=True
        ).astype(jnp.float32),
        lax.psum_scatter(
            audio_term.astype(jnp.bfloat16), ("mp", "sub"), scatter_dimension=1, tiled=True
        ).astype(jnp.float32),
    )
    video_out = (video_in.astype(jnp.float32) + video_sum).astype(jnp.bfloat16)
    audio_out = (audio_in.astype(jnp.float32) + audio_sum).astype(jnp.bfloat16)
    return (video_out, audio_out)


def solution(mesh):
    in_specs = (
        P(("groups", "seq"), ("mp", "sub")),
        P(("groups", "seq"), ("mp", "sub")),
        P(("groups", "seq"), ("mp", "sub")),
        P(("groups", "seq"), ("mp", "sub")),
        P(("groups", "seq"), ("mp", "sub")),
        P(("groups", "seq"), ("mp", "sub")),
        P(("groups", "seq"), ("mp", "sub")),
        P(("groups", "seq"), ("mp", "sub")),
        P(("groups", "seq"), ("mp", "sub")),
        P(("groups", "seq"), ("mp", "sub")),
        P(("groups", "seq"), ("mp", "sub")),
        P(("mp", "sub"), None),
        P(("mp", "sub"), None),
        P(("mp", "sub"), None),
        P(),
        P(),
        P(("groups", "seq")),
        P(("groups", "seq")),
        P("groups"),
    )
    out_specs = (P(("groups", "seq"), ("mp", "sub")), P(("groups", "seq"), ("mp", "sub")))
    return jax.shard_map(
        functools.partial(on_device, mesh), mesh=mesh, in_specs=in_specs, out_specs=out_specs, check_vma=False
    )
```

```python
import functools
import math

import jax
import jax.numpy as jnp
from jax import lax
from jax.experimental import pallas as pl
from jax.experimental.pallas import tpu as pltpu
from jax.sharding import PartitionSpec as P

DHV = 128
DHC = 64
NT = 16


def start_state(rows, heads, width):
    return (
        jnp.full((rows, heads), -1e30, jnp.float32),
        jnp.zeros((rows, heads), jnp.float32),
        jnp.zeros((rows, heads, width), jnp.float32),
    )


def update_block(state, queries, keys, values, heads, width, allowed):
    rows = queries.shape[0]
    count = keys.shape[0]
    q_heads = queries.reshape(rows, heads, width)
    k_heads = keys.reshape(count, heads, width)
    v_heads = values.reshape(count, heads, width)
    scores = jnp.einsum(
        "qhd,khd->qhk", q_heads, k_heads, preferred_element_type=jnp.float32
    ) / math.sqrt(width)
    if allowed is not None:
        scores = jnp.where(allowed[None, None, :], scores, -jnp.inf)
    peak_old, total_old, summed_old = state
    peak = jnp.maximum(peak_old, jnp.max(scores, axis=2))
    weights = jnp.exp(scores - peak[:, :, None])
    factor = jnp.exp(peak_old - peak)
    total = total_old * factor + jnp.sum(weights, axis=2)
    summed = summed_old * factor[:, :, None] + jnp.einsum(
        "qhk,khd->qhd", weights.astype(jnp.bfloat16), v_heads, preferred_element_type=jnp.float32
    )
    return (peak, total, summed)


def update_state(state, queries, keys, values, heads, width, start, limit):
    count = keys.shape[0]
    block = 1024 if count > 1024 and count % 1024 == 0 else count
    if block == count:
        allowed = None
        if limit is not None:
            allowed = jnp.arange(count, dtype=jnp.int32) < limit
        return update_block(state, queries, keys, values, heads, width, allowed)
    steps = count // block
    key_blocks = keys.reshape(steps, block, keys.shape[1])
    value_blocks = values.reshape(steps, block, values.shape[1])
    offsets = jnp.arange(steps, dtype=jnp.int32) * block

    def one_block(carry, items):
        key_rows, value_rows, offset = items
        allowed = None
        if limit is not None:
            allowed = start + offset + jnp.arange(block, dtype=jnp.int32) < limit
        return (update_block(carry, queries, key_rows, value_rows, heads, width, allowed), None)

    result, _ = lax.scan(one_block, state, (key_blocks, value_blocks, offsets))
    return result


def finish(state, heads, width):
    peak, total, summed = state
    rows = summed.shape[0]
    return (summed / total[:, :, None]).reshape(rows, heads * width).astype(jnp.bfloat16)


MESH = pl.DeviceIdType.MESH
BF16 = jnp.bfloat16
F32 = jnp.float32
CHUNKS = 1


def fits(mesh, q_self, q_a2v, k_a2v):
    seq = mesh.shape["seq"]
    return (
        seq > 1
        and q_self.shape[1] == seq * DHV
        and q_a2v.shape[1] == seq * DHC
        and 2 * DHC == DHV
        and seq % 2 == 0
        and k_a2v.shape[0] % 32 == 0
        and seq * q_self.shape[0] <= 1024
        and mesh.shape["sub"] == 2
        and mesh.shape["mp"] > 1
    )


def attend(queries, keys, values, width, allowed=None):
    scores = lax.dot_general(
        queries, keys, (((1,), (1,)), ((), ())), preferred_element_type=F32
    )
    if allowed is not None:
        scores = jnp.where(allowed, scores, -jnp.inf)
    peak = jnp.max(scores, axis=1, keepdims=True)
    weights = jnp.exp2((scores - peak) * (math.log2(math.e) / math.sqrt(width)))
    total = jnp.sum(weights, axis=1, keepdims=True)
    summed = jnp.dot(weights.astype(BF16), values, preferred_element_type=F32)
    return summed / total


def spread(hot, table):
    return lax.dot_general(hot, table, (((0,), (0,)), ((), ())), preferred_element_type=F32)


def kernel(
    seq,
    mp,
    video_in,
    audio_in,
    q_self,
    k_self,
    v_self,
    q_a2v,
    k_a2v,
    v_a2v,
    q_v2a,
    k_v2a,
    v_v2a,
    wo_self,
    wo_a2v,
    wo_v2a,
    video_gates,
    audio_gates,
    video_steps,
    audio_steps,
    audio_len,
    video_out,
    audio_out,
    qs,
    ks,
    vs,
    qa,
    ka,
    va,
    qv_in,
    kv_in,
    vv_in,
    q_pack,
    kv_pack,
    q_got,
    kv_got,
    os_send,
    os,
    ov_send,
    ov_got,
    ws,
    wa,
    wv,
    vg,
    ag,
    vin,
    ain,
    vsteps,
    asteps,
    alen,
    vout,
    aout,
    gain,
    term,
    core_send,
    core_got,
    kept,
    mp_send,
    mp_got,
    acore_send,
    acore_got,
    akept,
    amp_send,
    amp_got,
    local_sem,
    seq_send_sem,
    seq_recv_sem,
    core_send_sem,
    core_recv_sem,
    mp_send_sem,
    mp_recv_sem,
):
    me = lax.axis_index("seq")
    my_mp = lax.axis_index("mp")
    my_sub = lax.axis_index("sub")
    rows = q_self.shape[0]
    arows = k_a2v.shape[0]
    width_v = wo_self.shape[1]
    width_a = wo_v2a.shape[1]
    owned_v = width_v // (2 * mp)
    owned_a = width_a // (2 * mp)
    part = owned_v // CHUNKS

    def at(index, size):
        return pl.ds(pl.multiple_of(index * size, size), size)

    def peer(d):
        return lax.rem(me + d, seq)

    def other_mp(d):
        return lax.rem(my_mp + d, mp)

    local = []

    def bring(source, target):
        copy = pltpu.make_async_copy(source, target, local_sem.at[len(local)])
        copy.start()
        local.append(copy)
        return copy

    cross = [
        bring(q_v2a, qv_in),
        bring(k_v2a, kv_in),
        bring(v_v2a, vv_in),
    ]
    first = [
        bring(video_steps, vsteps),
        bring(audio_len, alen),
        bring(video_gates, vg),
        bring(q_a2v, qa),
        bring(k_a2v, ka.at[at(me, arows)]),
        bring(v_a2v, va.at[at(me, arows)]),
        bring(wo_a2v, wa),
    ]
    own = [
        bring(q_self.at[:, at(me, DHV)], qs.at[at(me, rows)]),
        bring(k_self.at[:, at(me, DHV)], ks.at[at(me, rows)]),
        bring(v_self.at[:, at(me, DHV)], vs.at[at(me, rows)]),
    ]
    late = [
        bring(wo_self, ws),
        bring(wo_v2a, wv),
        bring(audio_gates, ag),
        bring(audio_steps, asteps),
        bring(video_in, vin),
        bring(audio_in, ain),
    ]

    barrier = pltpu.get_barrier_semaphore()
    for d in range(1, seq):
        pl.semaphore_signal(barrier, inc=1, device_id={"seq": peer(d)}, device_id_type=MESH)
    pl.semaphore_signal(barrier, inc=1, device_id={"sub": 1 - my_sub}, device_id_type=MESH)
    for d in range(1, mp):
        pl.semaphore_signal(barrier, inc=1, device_id={"mp": other_mp(d)}, device_id_type=MESH)
    pl.semaphore_wait(barrier, seq - 1 + 1 + mp - 1)

    sent = []

    def to_seq(kind, d, source, target):
        copy = pltpu.make_async_remote_copy(
            src_ref=source,
            dst_ref=target,
            send_sem=seq_send_sem.at[kind, d],
            recv_sem=seq_recv_sem.at[kind, d],
            device_id={"seq": peer(d)},
            device_id_type=MESH,
        )
        copy.start()
        sent.append(copy)
        return copy

    order = [d for d in range(1, seq)]
    self_in = []
    for kind, (source, target) in enumerate(((k_self, ks), (q_self, qs), (v_self, vs))):
        for d in order:
            self_in.append(
                to_seq(kind, d, source.at[:, at(peer(d), DHV)], target.at[at(me, rows)])
            )
    a2v_in = []
    for kind, (source, target) in enumerate(((k_a2v, ka), (v_a2v, va))):
        for d in order:
            a2v_in.append(to_seq(3 + kind, d, source, target.at[at(me, arows)]))

    for copy in cross:
        copy.wait()
    half = arows // 2
    for h in range(seq):
        cols = slice(h * DHC, (h + 1) * DHC)
        kv = jnp.concatenate(
            [kv_in[:, cols].astype(F32), vv_in[:, cols].astype(F32)], axis=1
        ).astype(BF16)
        qh = qv_in[:, cols].astype(F32)
        kv_pack[h] = kv
        q_pack[h] = jnp.concatenate([qh[:half], qh[half:]], axis=1).astype(BF16)
    q_got[me] = q_pack[me]
    kv_got[at(me, rows), :] = kv_pack[me]

    for copy in first:
        copy.wait()
    picks = lax.broadcasted_iota(jnp.int32, (vg.shape[0], rows), 0)
    hot = (picks == vsteps[...]).astype(F32).astype(BF16)
    tile = min(512, width_v)
    for c in range(width_v // tile):
        cols = slice(c * tile, (c + 1) * tile)
        gain[:, cols] = spread(hot, vg[:, 0, cols]).astype(BF16)
    for copy in own:
        copy.wait()
    for copy in self_in:
        copy.wait_recv()
    self_back = []
    for d in order + [0]:
        out = attend(qs[at(peer(d), rows), :], ks[...], vs[...], DHV).astype(BF16)
        if d == 0:
            os[:, at(me, DHV)] = out
        else:
            os_send[d] = out
            self_back.append(to_seq(7, d, os_send.at[d], os.at[:, at(me, DHV)]))


    for copy in a2v_in:
        copy.wait_recv()
    count = seq * arows
    limit = alen[0]
    allowed = lax.broadcasted_iota(jnp.int32, (2 * rows, count), 1) < limit
    low = lax.broadcasted_iota(jnp.int32, (rows, 2 * DHC), 1) < DHC
    pieces = []
    for pair in range(seq // 2):
        cols = slice(pair * 2 * DHC, (pair + 1) * 2 * DHC)
        qp = qa[:, cols]
        zero = jnp.zeros_like(qp)
        both = jnp.concatenate([jnp.where(low, qp, zero), jnp.where(low, zero, qp)], axis=0)
        out = attend(both, ka[:, cols], va[:, cols], DHC, allowed)
        pieces.append(jnp.where(low, out[:rows], out[rows:]).astype(BF16))
    a2v_att = jnp.concatenate(pieces, axis=1)
    for c in range(width_v // tile):
        cols = slice(c * tile, (c + 1) * tile)
        term[:, cols] = spread(hot, vg[:, 1, cols]) * jnp.dot(
            a2v_att, wa[:, cols], preferred_element_type=F32
        )

    v2a_in = []
    for d in order:
        v2a_in.append(to_seq(5, d, q_pack.at[peer(d)], q_got.at[me]))
        v2a_in.append(to_seq(6, d, kv_pack.at[peer(d)], kv_got.at[at(me, rows)]))

    for copy in late:
        copy.wait()
    for copy in self_back:
        copy.wait_recv()
    self_att = os[...]

    def owner(m, s):
        return 2 * m + s

    def video_part(m, s, c):
        cols = pl.ds(pl.multiple_of(owner(m, s) * owned_v + c * part, part), part)
        return term[:, cols] + gain[:, cols].astype(F32) * jnp.dot(
            self_att, ws[:, cols], preferred_element_type=F32
        )

    def to_core(c, d, source, target):
        copy = pltpu.make_async_remote_copy(
            src_ref=source,
            dst_ref=target,
            send_sem=core_send_sem.at[c, d],
            recv_sem=core_recv_sem.at[c, d],
            device_id={"sub": 1 - my_sub},
            device_id_type=MESH,
        )
        copy.start()
        sent.append(copy)
        return copy

    def to_mp(c, d, source, target):
        copy = pltpu.make_async_remote_copy(
            src_ref=source,
            dst_ref=target,
            send_sem=mp_send_sem.at[c, d],
            recv_sem=mp_recv_sem.at[c, d],
            device_id={"mp": other_mp(d)},
            device_id_type=MESH,
        )
        copy.start()
        sent.append(copy)
        return copy

    core_copies = {}
    mp_copies = {}

    def exchange(c, d):
        core_send[c, d] = video_part(other_mp(d), 1 - my_sub, c).astype(BF16)
        core_copies[c, d] = to_core(c, d, core_send.at[c, d], core_got.at[c, d])
        kept[c, d] = video_part(other_mp(d), my_sub, c)

    def pass_on(c):
        for d in range(1, mp):
            core_copies[c, d].wait_recv()
            mp_send[c, d] = (kept[c, d] + core_got[c, d].astype(F32)).astype(BF16)
            mp_copies[c, d] = to_mp(c, d, mp_send.at[c, d], mp_got.at[c, d])

    for c in range(CHUNKS):
        for d in range(1, mp):
            exchange(c, d)
        if c > 0:
            pass_on(c - 1)
    pass_on(CHUNKS - 1)

    for copy in v2a_in:
        copy.wait_recv()
    blocks = []
    for p in range(seq):
        got = q_got[p].astype(F32)
        blocks.append(got[:, :DHC])
        blocks.append(got[:, DHC:])
    qv = jnp.concatenate(blocks, axis=0)
    qv = jnp.concatenate([qv, jnp.zeros_like(qv)], axis=1).astype(BF16)
    out = attend(qv, kv_got[...], kv_got[...], DHC)[:, DHC:]
    for p in range(seq):
        top = out[p * arows : p * arows + half]
        bottom = out[p * arows + half : (p + 1) * arows]
        ov_send[p] = jnp.concatenate([top, bottom], axis=1).astype(BF16)
    v2a_back = []
    for d in order:
        v2a_back.append(to_seq(8, d, ov_send.at[peer(d)], ov_got.at[me]))
    ov_got[me] = ov_send[me]

    for c in range(CHUNKS):
        exchange(c, 0)

    for copy in v2a_back:
        copy.wait_recv()
    blocks = []
    for h in range(seq):
        got = ov_got[h].astype(F32)
        blocks.append(jnp.concatenate([got[:, :DHC], got[:, DHC:]], axis=0))
    v2a_att = jnp.concatenate(blocks, axis=1).astype(BF16)
    apicks = lax.broadcasted_iota(jnp.int32, (ag.shape[0], arows), 0)
    hot_audio = (apicks == asteps[...]).astype(F32).astype(BF16)
    positions = me * arows + lax.broadcasted_iota(jnp.int32, (arows, owned_a), 0)
    present = (positions < limit).astype(F32)

    def audio_part(m, s):
        cols = at(owner(m, s), owned_a)
        return (
            present
            * spread(hot_audio, ag[:, cols])
            * jnp.dot(v2a_att, wv[:, cols], preferred_element_type=F32)
        )

    for d in range(mp):
        acore_send[d] = audio_part(other_mp(d), 1 - my_sub).astype(BF16)
    acore = to_core(CHUNKS, 0, acore_send, acore_got)
    for d in range(mp):
        akept[d] = audio_part(other_mp(d), my_sub)
    acore.wait_recv()
    for d in range(1, mp):
        amp_send[d] = (akept[d] + acore_got[d].astype(F32)).astype(BF16)
        mp_copies[CHUNKS, d] = to_mp(CHUNKS, d, amp_send.at[d], amp_got.at[d])

    results = []
    for c in range(CHUNKS):
        cols = slice(c * part, (c + 1) * part)
        core_copies[c, 0].wait_recv()
        total = kept[c, 0] + core_got[c, 0].astype(F32)
        for d in range(1, mp):
            mp_copies[c, d].wait_recv()
            total = total + mp_got[c, d].astype(F32)
        vout[:, cols] = (vin[:, cols].astype(F32) + total).astype(BF16)
        results.append(bring(vout.at[:, cols], video_out.at[:, cols]))
    total = akept[0] + acore_got[0].astype(F32)
    for d in range(1, mp):
        mp_copies[CHUNKS, d].wait_recv()
        total = total + amp_got[d].astype(F32)
    aout[...] = (ain[...].astype(F32) + total).astype(BF16)
    results.append(bring(aout, audio_out))
    for copy in results:
        copy.wait()
    for copy in sent:
        copy.wait_send()


def fused(mesh, *args):
    (
        video_in,
        audio_in,
        q_self,
        _,
        _,
        q_a2v,
        k_a2v,
        _,
        q_v2a,
        k_v2a,
        _,
        wo_self,
        wo_a2v,
        wo_v2a,
        video_gates,
        audio_gates,
        video_steps,
        audio_steps,
        _,
    ) = args
    seq, mp = mesh.shape["seq"], mesh.shape["mp"]
    rows, arows = q_self.shape[0], k_a2v.shape[0]
    args = list(args)
    args[16] = video_steps.reshape(1, rows)
    args[17] = audio_steps.reshape(1, arows)
    part = video_in.shape[1] // CHUNKS
    owned_a = audio_in.shape[1]

    def buffer(*shape, dtype=BF16):
        return pltpu.VMEM(shape, dtype)

    like = lambda array: pltpu.VMEM(array.shape, array.dtype)
    scratch = [
        buffer(seq * rows, DHV),
        buffer(seq * rows, DHV),
        buffer(seq * rows, DHV),
        like(q_a2v),
        buffer(seq * arows, seq * DHC),
        buffer(seq * arows, seq * DHC),
        like(q_v2a),
        like(k_v2a),
        like(k_v2a),
        buffer(seq, arows // 2, 2 * DHC),
        buffer(seq, rows, 2 * DHC),
        buffer(seq, arows // 2, 2 * DHC),
        buffer(seq * rows, 2 * DHC),
        buffer(seq, rows, DHV),
        buffer(rows, seq * DHV),
        buffer(seq, arows // 2, 2 * DHC),
        buffer(seq, arows // 2, 2 * DHC),
        like(wo_self),
        like(wo_a2v),
        like(wo_v2a),
        like(video_gates),
        like(audio_gates),
        like(video_in),
        like(audio_in),
        buffer(1, rows, dtype=jnp.int32),
        buffer(1, arows, dtype=jnp.int32),
        pltpu.SMEM((1,), jnp.int32),
        like(video_in),
        like(audio_in),
        buffer(rows, wo_self.shape[1]),
        buffer(rows, wo_self.shape[1], dtype=F32),
        buffer(CHUNKS, mp, rows, part),
        buffer(CHUNKS, mp, rows, part),
        buffer(CHUNKS, mp, rows, part, dtype=F32),
        buffer(CHUNKS, mp, rows, part),
        buffer(CHUNKS, mp, rows, part),
        buffer(mp, arows, owned_a),
        buffer(mp, arows, owned_a),
        buffer(mp, arows, owned_a, dtype=F32),
        buffer(mp, arows, owned_a),
        buffer(mp, arows, owned_a),
        pltpu.SemaphoreType.DMA((32,)),
        pltpu.SemaphoreType.DMA((9, seq)),
        pltpu.SemaphoreType.DMA((9, seq)),
        pltpu.SemaphoreType.DMA((CHUNKS + 1, mp)),
        pltpu.SemaphoreType.DMA((CHUNKS + 1, mp)),
        pltpu.SemaphoreType.DMA((CHUNKS + 1, mp)),
        pltpu.SemaphoreType.DMA((CHUNKS + 1, mp)),
    ]
    anywhere = pl.BlockSpec(memory_space=pltpu.HBM)
    return pl.pallas_call(
        functools.partial(kernel, seq, mp),
        out_shape=(
            jax.ShapeDtypeStruct(video_in.shape, video_in.dtype),
            jax.ShapeDtypeStruct(audio_in.shape, audio_in.dtype),
        ),
        in_specs=[anywhere] * len(args),
        out_specs=(anywhere, anywhere),
        scratch_shapes=scratch,
        compiler_params=pltpu.CompilerParams(
            collective_id=0, has_side_effects=True, vmem_limit_bytes=63 * 1024 * 1024
        ),
    )(*args)


def on_device(
    mesh,
    video_in,
    audio_in,
    q_self,
    k_self,
    v_self,
    q_a2v,
    k_a2v,
    v_a2v,
    q_v2a,
    k_v2a,
    v_v2a,
    wo_self,
    wo_a2v,
    wo_v2a,
    video_gates,
    audio_gates,
    video_steps,
    audio_steps,
    audio_len,
):
    if fits(mesh, q_self, q_a2v, k_a2v):
        return fused(
            mesh,
            video_in,
            audio_in,
            q_self,
            k_self,
            v_self,
            q_a2v,
            k_a2v,
            v_a2v,
            q_v2a,
            k_v2a,
            v_v2a,
            wo_self,
            wo_a2v,
            wo_v2a,
            video_gates,
            audio_gates,
            video_steps,
            audio_steps,
            audio_len,
        )
    heads_self = q_self.shape[1] // DHV
    heads_cross = q_a2v.shape[1] // DHC
    rows_video = q_self.shape[0]
    rows_audio = q_v2a.shape[0]
    limit = audio_len[0]
    piece = (
        lax.all_gather(k_a2v, "seq", axis=0, tiled=True),
        lax.all_gather(v_a2v, "seq", axis=0, tiled=True),
    )
    a2v_state = update_state(
        start_state(rows_video, heads_cross, DHC),
        q_a2v,
        piece[0],
        piece[1],
        heads_cross,
        DHC,
        jnp.int32(0),
        limit,
    )
    a2v_att = finish(a2v_state, heads_cross, DHC)
    piece = (
        lax.all_gather(k_self, "seq", axis=0, tiled=True),
        lax.all_gather(v_self, "seq", axis=0, tiled=True),
    )
    self_state = update_state(
        start_state(rows_video, heads_self, DHV),
        q_self,
        piece[0],
        piece[1],
        heads_self,
        DHV,
        jnp.int32(0),
        None,
    )
    piece = (
        lax.all_gather(k_v2a, "seq", axis=0, tiled=True),
        lax.all_gather(v_v2a, "seq", axis=0, tiled=True),
    )
    v2a_state = update_state(
        start_state(rows_audio, heads_cross, DHC),
        q_v2a,
        piece[0],
        piece[1],
        heads_cross,
        DHC,
        jnp.int32(0),
        None,
    )
    self_att = finish(self_state, heads_self, DHV)
    v2a_att = finish(v2a_state, heads_cross, DHC)
    levels = jnp.arange(NT, dtype=jnp.int32)
    video_hot = (video_steps[:, None] == levels[None, :]).astype(jnp.bfloat16)
    video_gain = jnp.dot(video_hot, video_gates.reshape(NT, -1), preferred_element_type=jnp.float32)
    width_video = video_gates.shape[2]
    video_term = video_gain[:, :width_video] * jnp.dot(
        self_att, wo_self, preferred_element_type=jnp.float32
    )
    video_term = video_term + video_gain[:, width_video:] * jnp.dot(
        a2v_att, wo_a2v, preferred_element_type=jnp.float32
    )
    audio_hot = (audio_steps[:, None] == levels[None, :]).astype(jnp.bfloat16)
    audio_gain = jnp.dot(audio_hot, audio_gates, preferred_element_type=jnp.float32)
    positions = lax.axis_index("seq") * rows_audio + jnp.arange(rows_audio, dtype=jnp.int32)
    present = (positions < limit).astype(jnp.float32)
    audio_term = (
        present[:, None] * audio_gain * jnp.dot(v2a_att, wo_v2a, preferred_element_type=jnp.float32)
    )
    video_sum, audio_sum = (
        lax.psum_scatter(
            video_term.astype(jnp.bfloat16), ("mp", "sub"), scatter_dimension=1, tiled=True
        ).astype(jnp.float32),
        lax.psum_scatter(
            audio_term.astype(jnp.bfloat16), ("mp", "sub"), scatter_dimension=1, tiled=True
        ).astype(jnp.float32),
    )
    video_out = (video_in.astype(jnp.float32) + video_sum).astype(jnp.bfloat16)
    audio_out = (audio_in.astype(jnp.float32) + audio_sum).astype(jnp.bfloat16)
    return (video_out, audio_out)


def solution(mesh):
    in_specs = (
        P(("groups", "seq"), ("mp", "sub")),
        P(("groups", "seq"), ("mp", "sub")),
        P(("groups", "seq"), ("mp", "sub")),
        P(("groups", "seq"), ("mp", "sub")),
        P(("groups", "seq"), ("mp", "sub")),
        P(("groups", "seq"), ("mp", "sub")),
        P(("groups", "seq"), ("mp", "sub")),
        P(("groups", "seq"), ("mp", "sub")),
        P(("groups", "seq"), ("mp", "sub")),
        P(("groups", "seq"), ("mp", "sub")),
        P(("groups", "seq"), ("mp", "sub")),
        P(("mp", "sub"), None),
        P(("mp", "sub"), None),
        P(("mp", "sub"), None),
        P(),
        P(),
        P(("groups", "seq")),
        P(("groups", "seq")),
        P("groups"),
    )
    out_specs = (P(("groups", "seq"), ("mp", "sub")), P(("groups", "seq"), ("mp", "sub")))
    return jax.shard_map(
        functools.partial(on_device, mesh), mesh=mesh, in_specs=in_specs, out_specs=out_specs, check_vma=False
    )
```
